32 devices in a mesh: rep: 8 (over y, x, core), fsdp: 4 (over z).
Axes of the slice: x: 2, y: 2, z: 4, core: 2. Of those that a mesh axis runs over, the one named last changes fastest.
Arguments:
- tokens: bfloat16 [4096, 8192], P(('rep', 'fsdp')), may hold values from -6 to 6
- grad_out: bfloat16 [4096, 128], P(('rep', 'fsdp')), may hold values from -0.25 to 0.25
- moment: float32 [8, 8192, 128], P('rep', 'fsdp'), may hold values from -6 to 6
- weight: bfloat16 [8192, 128], P('fsdp'), may hold values from -0.0625 to 0.0625
- next_tokens: bfloat16 [4096, 8192], P(('rep', 'fsdp')), may hold values from -6 to 6
- index: int32 [8, 128, 2, 32], P('rep', 'fsdp'), may hold values from 0 to 4095, as said below
Outputs:
- update: float32 [8192, 128], P('fsdp')
- new_moment: float32 [8, 8192, 128], P('rep', 'fsdp')
- next_out: bfloat16 [4096, 128], P(('rep', 'fsdp'))
The draws below stay inside these ranges and needn't reach their ends.
Inputs may be any that keep to these rules, and one draw needn't show every extreme that they name: `index`: for each replica and tile the 32 positions are distinct; position p stands for row p // 64 and column p % 64 of the tile.
All inputs are finite; a program needn't handle non-finite values.
Results may differ from the reference program's by a relative error of at most 0.008.
Values may be sent and summed in bfloat16 or wider, within the bound.
No kernel may reach another device: no remote copies, remote signals or barrier semaphores. Data moves between devices by JAX's collectives and lax.ppermute only.
A program may use at most 64 MiB of HBM per device.

```python
import jax
import jax.numpy as jnp
from jax import lax

D = 8192
OUT = 128
TILE = 64
K = 32
TOK_DEV = 128
TOKENS = 4096
N_REP = 8
N_FSDP = 4


def draw_index(key, part):
    key = jax.random.fold_in(key, 7)
    tile_count = N_REP * (D // TILE) * (OUT // TILE)
    keys = jax.random.split(key, tile_count)
    positions = TILE * TILE

    def one_tile(tile_key):
        scores = jax.random.randint(tile_key, (positions,), 0, 2 ** 18) * positions + jnp.arange(positions, dtype=jnp.int32)
        return lax.top_k(scores, K)[1].astype(jnp.int32)
    picked = lax.map(one_tile, keys)
    return picked.reshape(N_REP, D // TILE, OUT // TILE, K)


def levels(stream_key, shape, pieces, least, top_value):
    level = 1.0
    for position, shards_of in pieces:
        steps = jax.random.uniform(jax.random.fold_in(jax.random.fold_in(stream_key, 6), position), (shards_of,), jnp.float32, least / len(pieces), top_value / len(pieces))
        level = level * jnp.repeat(jnp.exp(steps), shape[position] // shards_of).reshape((-1,) + (1,) * (len(shape) - 1 - position))
    return level


def noise(stream_key, shape, spread, reach, shards=(), held_as=jnp.bfloat16):
    values = jax.random.normal(stream_key, shape, jnp.float32) * spread
    if len(shards) > 0:
        values = levels(stream_key, shape, shards, -0.22, 0.18) * values
    return jnp.clip(values, min=-reach, max=reach).astype(held_as)


def setup_inputs(seed: int = 0) -> dict:
    splits = jax.random.split(jax.random.key(seed), 7)
    tokens = noise(splits[0], (TOKENS, D), 1.0, 6.0, ((0, 32),))
    grad_out = noise(splits[1], (TOKENS, OUT), (TOK_DEV * N_FSDP) ** -0.5, 0.25, ((0, 32),))
    moment = noise(splits[2], (N_REP, D, OUT), 1.0, 6.0, ((0, 8), (1, 4)), jnp.float32)
    weight = noise(splits[3], (D, OUT), D ** -0.5, 0.0625, ((0, 4),))
    next_tokens = noise(splits[4], (TOKENS, D), 1.0, 6.0, ((0, 32),))
    index = draw_index(jax.random.fold_in(splits[6], 71), 0)
    return {"tokens": tokens, "grad_out": grad_out, "moment": moment, "weight": weight, "next_tokens": next_tokens, "index": index}


momentum_decay = 0.999
step_size = 0.005

def cosine_table(order):
    freq = jnp.arange(order, dtype=jnp.float32)[:, None]
    place = jnp.arange(order, dtype=jnp.float32)[None, :]
    table = jnp.sqrt(2.0 / order) * jnp.cos(jnp.pi * (2.0 * place + 1.0) * freq / (2.0 * order))
    return table * jnp.where(freq == 0.0, jnp.sqrt(0.5), 1.0)

def forward_tiles(field, table):
    side = table.shape[0]
    shard_rows, width = field.shape
    tiles = field.reshape(shard_rows // side, side, width)
    along = jnp.einsum('ab,ibc->iac', table, tiles, precision=lax.Precision.HIGHEST)
    block = jnp.kron(jnp.eye(width // side, dtype=jnp.float32), table.T)
    return jnp.matmul(along, block, precision=lax.Precision.HIGHEST)

def inverse_tiles(spectra, table):
    side = table.shape[0]
    width = spectra.shape[2]
    along = jnp.einsum('ab,iac->ibc', table, spectra, precision=lax.Precision.HIGHEST)
    block = jnp.kron(jnp.eye(width // side, dtype=jnp.float32), table)
    result = jnp.matmul(along, block, precision=lax.Precision.HIGHEST)
    return result.reshape(spectra.shape[0] * side, width)

def one_hots(places, side, width):
    row_of = places // side
    col_of = places % side + jnp.arange(width // side, dtype=jnp.int32)[:, None] * side
    row_hot = (row_of[..., None] == jnp.arange(side, dtype=jnp.int32)).astype(jnp.float32)
    col_hot = (col_of[..., None] == jnp.arange(width, dtype=jnp.int32)).astype(jnp.float32)
    return (row_hot, col_hot)

def select_values(spectra, row_hot, col_hot):
    picked = jnp.einsum('ijka,iac->ijkc', row_hot, spectra, precision=lax.Precision.HIGHEST)
    return lax.optimization_barrier(jnp.sum(picked * col_hot, axis=-1))

def densify(sent_values, row_hot, col_hot):
    return jnp.einsum('ijka,ijkc->iac', row_hot * sent_values[..., None], col_hot, precision=lax.Precision.HIGHEST)

def reference(tokens, grad_out, moment, weight, next_tokens, index):
    table = cosine_table(TILE)
    grouped = tokens.reshape(N_REP, N_FSDP, TOK_DEV, D)
    grouped_grad = grad_out.reshape(N_REP, N_FSDP, TOK_DEV, OUT)

    def one_replica(total, packed):
        inputs, outgrad, moment_old, places = packed
        partial_value = jnp.einsum('ftd,fto->fdo', inputs.astype(jnp.float32), outgrad.astype(jnp.float32), precision=lax.Precision.HIGHEST)
        rounded = lax.optimization_barrier(partial_value.astype(jnp.bfloat16))
        grad = lax.optimization_barrier(jnp.sum(rounded.astype(jnp.float32), axis=0))
        moment_now = momentum_decay * moment_old + grad
        spectra = forward_tiles(moment_now, table)
        row_hot, col_hot = one_hots(places, TILE, OUT)
        sent_values = select_values(spectra, row_hot, col_hot)
        dense = densify(sent_values, row_hot, col_hot)
        return (total + dense, moment_now - inverse_tiles(dense, table))
    start_total = jnp.zeros((D // TILE, TILE, OUT), jnp.float32)
    total, new_moment = lax.scan(one_replica, start_total, (grouped, grouped_grad, moment, index))
    update = inverse_tiles(total, table)
    new_weight = (weight.astype(jnp.float32) - step_size * update).astype(jnp.bfloat16)
    next_out = jnp.dot(next_tokens, new_weight, preferred_element_type=jnp.float32).astype(jnp.bfloat16)
    return (update, new_moment, next_out)
```

```python
import functools

import jax
import jax.numpy as jnp
import numpy as np
from jax import lax
from jax.experimental import pallas as pl
from jax.experimental.pallas import tpu as pltpu
from jax.sharding import PartitionSpec as P

TILE = 64
LANES = 128

momentum_decay = 0.999
step_size = 0.005


def cosine_array(order):
    freq = np.arange(order, dtype=np.float64)[:, None]
    place = np.arange(order, dtype=np.float64)[None, :]
    table = np.sqrt(2.0 / order) * np.cos(np.pi * (2.0 * place + 1.0) * freq / (2.0 * order))
    return table * np.where(freq == 0.0, np.sqrt(0.5), 1.0)


def tables():
    block = np.kron(np.eye(2), cosine_array(TILE)).astype(np.float32)
    high = block.astype(jnp.bfloat16)
    low = (block - high.astype(np.float32)).astype(jnp.bfloat16)
    inv = np.concatenate([high.T, low.T], axis=0)
    fwd = np.concatenate([high, low], axis=0)
    return jnp.asarray(inv), jnp.asarray(fwd)


def split(x):
    high = x.astype(jnp.bfloat16)
    return high, (x - high.astype(jnp.float32)).astype(jnp.bfloat16)


def dot(a, b, contract=((1,), (0,))):
    return lax.dot_general(a, b, (contract, ((), ())), preferred_element_type=jnp.float32)


def hot(row, fill):
    return jnp.where(lax.broadcasted_iota(jnp.int32, (LANES, LANES), 0) == row, fill, 0.0)


def partial_kernel(slots, tok, grad, *outs):
    for i, out in enumerate(outs):

        @pl.when(pl.program_id(0) == i)
        def _():
            out[...] = dot(tok[...], grad[...], ((0,), (0,))).astype(out.dtype)


def partial_chunks(tokens, grad_out, slots, rows):
    count = slots.shape[0]
    width = grad_out.shape[1]
    toks = tokens.shape[0]
    return pl.pallas_call(
        partial_kernel,
        grid_spec=pltpu.PrefetchScalarGridSpec(
            num_scalar_prefetch=1,
            grid=(count,),
            in_specs=[
                pl.BlockSpec((toks, rows), lambda s, slots: (0, slots[s])),
                pl.BlockSpec((toks, width), lambda s, slots: (0, 0)),
            ],
            out_specs=[pl.BlockSpec((rows, width), lambda s, slots: (0, 0)) for _ in range(count)],
        ),
        out_shape=[jax.ShapeDtypeStruct((rows, width), jnp.bfloat16) for _ in range(count)],
        cost_estimate=pl.CostEstimate(
            flops=2 * count * rows * width * toks, bytes_accessed=count * rows * (width + toks) * 2, transcendentals=0
        ),
        compiler_params=pltpu.CompilerParams(vmem_limit_bytes=32 * 2**20),
    )(slots, tokens, grad_out)


def entry_rows(inv, row, col):
    hots = jnp.concatenate([hot(row, 1.0), hot(col, 1.0)], axis=1).astype(jnp.bfloat16)
    both = dot(inv, hots)
    return both[:LANES, :LANES], both[LANES:, :LANES], both[:LANES, LANES:], both[LANES:, LANES:]


def select_kernel(groups, me, inv_ref, idx_ref, tok_ref, grad_ref, moment_ref, out_ref):
    inv = inv_ref[...]
    grad = grad_ref[...]

    def group(g, own):
        row = idx_ref[0, 0, pl.ds(g, 1), :]
        col = idx_ref[0, 1, pl.ds(g, 1), :]
        a_hi, a_lo, b_hi, b_lo = entry_rows(inv, row, col)
        a2 = jnp.concatenate([a_hi, a_lo], axis=1).astype(jnp.bfloat16)
        b2 = jnp.concatenate([b_hi, b_lo], axis=1).astype(jnp.bfloat16)
        tok = tok_ref[:, pl.ds(pl.multiple_of(g * LANES, LANES), LANES)]
        ta = dot(tok, a2)
        gb = dot(grad, b2)
        value = jnp.sum((ta[:, :LANES] + ta[:, LANES:]) * (gb[:, :LANES] + gb[:, LANES:]), axis=0, keepdims=True)
        if own:
            m_hi, m_lo = split(momentum_decay * moment_ref[pl.ds(pl.multiple_of(g * LANES, LANES), LANES), :])
            mb = dot(m_hi, b2)
            mb = mb[:, :LANES] + mb[:, LANES:] + dot(m_lo, b2[:, :LANES])
            value = value + jnp.sum(mb * (a_hi + a_lo), axis=0, keepdims=True)
        out_ref[0, pl.ds(g, 1), :] = value

    @pl.when(pl.program_id(0) == 0)
    def _():
        for g in range(groups):
            group(g, True)

    @pl.when(pl.program_id(0) != 0)
    def _():
        for g in range(groups):
            group(g, False)


def select_values(me, inv, idx, tokens, grad_out, moment):
    n_f, _, groups, _ = idx.shape
    rows = groups * LANES
    toks = tokens.shape[0]
    width = grad_out.shape[1]
    return pl.pallas_call(
        functools.partial(select_kernel, groups),
        grid_spec=pltpu.PrefetchScalarGridSpec(
            num_scalar_prefetch=1,
            grid=(n_f,),
            in_specs=[
                pl.BlockSpec(inv.shape, lambda s, me: (0, 0)),
                pl.BlockSpec((1, 2, groups, LANES), lambda s, me: (s, 0, 0, 0)),
                pl.BlockSpec((toks, rows), lambda s, me: (0, me[0] ^ s)),
                pl.BlockSpec((toks, width), lambda s, me: (0, 0)),
                pl.BlockSpec((rows, width), lambda s, me: (0, 0)),
            ],
            out_specs=pl.BlockSpec((1, groups, LANES), lambda s, me: (me[0] ^ s, 0, 0)),
        ),
        out_shape=jax.ShapeDtypeStruct((n_f, groups, LANES), jnp.float32),
        cost_estimate=pl.CostEstimate(
            flops=2 * n_f * groups * LANES**3 * 6, bytes_accessed=4 * 2**20, transcendentals=0
        ),
        compiler_params=pltpu.CompilerParams(vmem_limit_bytes=32 * 2**20),
    )(me, inv, idx, tokens, grad_out, moment)


def base_kernel(groups, inv_ref, idx_ref, val_ref, moment_ref, out_ref):
    inv = inv_ref[...]
    for g in range(groups):
        a_hi, a_lo, b_hi, b_lo = entry_rows(inv, idx_ref[0, 0, g : g + 1, :], idx_ref[0, 1, g : g + 1, :])
        av_hi, av_lo = split((a_hi + a_lo) * val_ref[g : g + 1, :])
        left = jnp.concatenate([av_hi, av_hi, av_lo], axis=1)
        right = jnp.concatenate([b_hi, b_lo, b_hi], axis=1).astype(jnp.bfloat16)
        part = slice(g * LANES, (g + 1) * LANES)
        out_ref[part, :] = momentum_decay * moment_ref[part, :] - dot(left, right, ((1,), (1,)))


def moment_base(inv, idx, values, moment):
    groups = values.shape[0]
    rows, width = moment.shape
    return pl.pallas_call(
        functools.partial(base_kernel, groups),
        grid=(1,),
        in_specs=[
            pl.BlockSpec(inv.shape, lambda i: (0, 0)),
            pl.BlockSpec((1, 2, groups, LANES), lambda i: (0, 0, 0, 0)),
            pl.BlockSpec((groups, LANES), lambda i: (0, 0)),
            pl.BlockSpec((rows, width), lambda i: (0, 0)),
        ],
        out_specs=pl.BlockSpec((rows, width), lambda i: (0, 0)),
        out_shape=jax.ShapeDtypeStruct((rows, width), jnp.float32),
        cost_estimate=pl.CostEstimate(
            flops=2 * groups * LANES**3 * 7, bytes_accessed=2 * rows * width * 4, transcendentals=0
        ),
        compiler_params=pltpu.CompilerParams(vmem_limit_bytes=32 * 2**20),
    )(inv, idx, values, moment)


def project_kernel(pieces, extra, place, inv_ref, nt_ref, here_ref, there_ref, out_ref, coef_ref):
    width = nt_ref.shape[1]
    total = jnp.zeros(out_ref.shape, jnp.float32)
    half = here_ref.shape[0]
    size = width // pieces
    for p in range(pieces):
        source = here_ref if p < half else there_ref
        cols = pl.ds(pl.multiple_of(place[p] * size, size), size)
        total += dot(nt_ref[:, cols], source[p % half, extra:, :])
    out_ref[...] = total
    inv = inv_ref[...]
    table = jnp.concatenate([inv[:LANES], inv[LANES:]], axis=1)
    for g in range(width // LANES):
        part = slice(g * LANES, (g + 1) * LANES)
        both = dot(nt_ref[:, part], table)
        coef_ref[:, part] = (both[:, :LANES] + both[:, LANES:]).astype(jnp.bfloat16)


def project(place, inv, next_tokens, here, there, extra):
    pieces = place.shape[0]
    toks, width = next_tokens.shape
    out = here.shape[2]
    full = lambda *shape: pl.BlockSpec(shape, lambda i, place: (0,) * len(shape))
    return pl.pallas_call(
        functools.partial(project_kernel, pieces, extra),
        grid_spec=pltpu.PrefetchScalarGridSpec(
            num_scalar_prefetch=1,
            grid=(1,),
            in_specs=[full(*inv.shape), full(toks, width), full(*here.shape), full(*there.shape)],
            out_specs=[full(toks, out), full(toks, width)],
        ),
        out_shape=[jax.ShapeDtypeStruct((toks, out), jnp.float32), jax.ShapeDtypeStruct((toks, width), jnp.bfloat16)],
        cost_estimate=pl.CostEstimate(
            flops=2 * toks * width * out * 3, bytes_accessed=6 * toks * width * 2, transcendentals=0
        ),
        compiler_params=pltpu.CompilerParams(vmem_limit_bytes=48 * 2**20),
    )(place, inv, next_tokens, here, there)


def total_kernel(groups, n_r, me, inv_ref, fwd_ref, idx_ref, val_ref, coef_ref, base_ref, up_ref, out_ref, acc_ref):
    step = pl.program_id(0)
    inv = inv_ref[...]
    fwd = fwd_ref[...]

    @pl.when(step == 0)
    def _():
        acc_ref[...] = jnp.zeros_like(acc_ref)

    def group(g, own):
        left, right = [], []
        for r in range(n_r):
            left.append(hot(idx_ref[r, 0, 0, pl.ds(g, 1), :], 1.0).astype(jnp.bfloat16))
            right.append(hot(idx_ref[r, 0, 1, pl.ds(g, 1), :], val_ref[r, 0, pl.ds(g, 1), :]).astype(jnp.bfloat16))
        dense = dot(jnp.concatenate(left, axis=1), jnp.concatenate(right, axis=1), ((1,), (1,)))
        q_hi, q_lo = split(dense)
        cols = pl.ds(pl.multiple_of(g * LANES, LANES), LANES)
        both = dot(coef_ref[:, cols], jnp.concatenate([q_hi, q_lo], axis=1))
        acc_ref[...] += both[:, :LANES] + both[:, LANES:]
        if own:
            c_hi, c_lo = inv[:LANES], inv[LANES:]
            along = dot(
                jnp.concatenate([c_hi, c_hi, c_lo], axis=1), jnp.concatenate([q_hi, q_lo, q_hi], axis=0)
            )
            s_hi, s_lo = split(along)
            f_hi, f_lo = fwd[:LANES], fwd[LANES:]
            up_ref[cols, :] = dot(
                jnp.concatenate([s_hi, s_hi, s_lo], axis=1), jnp.concatenate([f_hi, f_lo, f_hi], axis=0)
            )

    @pl.when(step == 0)
    def _():
        @pl.loop(0, groups)
        def _(g):
            group(g, True)

    @pl.when(step != 0)
    def _():
        @pl.loop(0, groups)
        def _(g):
            group(g, False)

    @pl.when(step == pl.num_programs(0) - 1)
    def _():
        s_hi, s_lo = split(acc_ref[...])
        f_hi, f_lo = fwd[:LANES], fwd[LANES:]
        moved = dot(jnp.concatenate([s_hi, s_hi, s_lo], axis=1), jnp.concatenate([f_hi, f_lo, f_hi], axis=0))
        out_ref[...] = (base_ref[...] - step_size * moved).astype(out_ref.dtype)


def totals(me, inv, fwd, idx, values, coef, base):
    n_r, n_f, _, groups, _ = idx.shape
    rows = groups * LANES
    toks, width = base.shape
    return pl.pallas_call(
        functools.partial(total_kernel, groups, n_r),
        grid_spec=pltpu.PrefetchScalarGridSpec(
            num_scalar_prefetch=1,
            grid=(n_f,),
            in_specs=[
                pl.BlockSpec(inv.shape, lambda s, me: (0, 0)),
                pl.BlockSpec(fwd.shape, lambda s, me: (0, 0)),
                pl.BlockSpec((n_r, 1, 2, groups, LANES), lambda s, me: (0, s, 0, 0, 0)),
                pl.BlockSpec((n_r, 1, groups, LANES), lambda s, me: (0, me[0] ^ s, 0, 0)),
                pl.BlockSpec((toks, rows), lambda s, me: (0, me[0] ^ s)),
                pl.BlockSpec((toks, width), lambda s, me: (0, 0)),
            ],
            out_specs=[
                pl.BlockSpec((rows, width), lambda s, me: (0, 0)),
                pl.BlockSpec((toks, width), lambda s, me: (0, 0)),
            ],
            scratch_shapes=[pltpu.VMEM((toks, width), jnp.float32)],
        ),
        out_shape=[
            jax.ShapeDtypeStruct((rows, width), jnp.float32),
            jax.ShapeDtypeStruct((toks, width), jnp.bfloat16),
        ],
        cost_estimate=pl.CostEstimate(
            flops=2 * n_f * groups * LANES**3 * (n_r + 2), bytes_accessed=4 * 2**20, transcendentals=0
        ),
        compiler_params=pltpu.CompilerParams(vmem_limit_bytes=32 * 2**20),
    )(me, inv, fwd, idx, values, coef, base)


def swap(x, axis, size, mask):
    return lax.ppermute(x, axis, [(i, i ^ mask) for i in range(size)])


SLOTS = np.array([[3, 1, 2, 0], [2, 0, 3, 1], [3, 1, 0, 2], [2, 0, 1, 3]], np.int32)


def line_fast(n_r, n_f, tokens, grad_out, moment, weight, next_tokens, index):
    bf16 = jnp.bfloat16
    r, f = lax.axis_index("rep"), lax.axis_index("fsdp")
    me = jnp.stack([f]).astype(jnp.int32)
    inv, fwd = tables()
    moment = moment[0]
    rows = moment.shape[0]
    groups = rows // LANES
    slice_rows = rows // n_r

    flat = index[0].reshape(groups, LANES)
    lane = jnp.arange(LANES, dtype=jnp.int32)
    row_pos = flat // TILE + (lane // TILE) * TILE
    col_pos = flat % TILE + (lane // (TILE // 2)) % 2 * TILE
    own_idx = jnp.concatenate([row_pos, col_pos], axis=0).astype(bf16)
    extra = own_idx.shape[0]
    share = lax.dynamic_slice_in_dim(weight, r * slice_rows, slice_rows, axis=0)
    held = jnp.concatenate([own_idx, share], axis=0)[None]

    slots = jnp.asarray(SLOTS)[f]
    first, second = partial_chunks(tokens, grad_out, slots[:2], rows)
    third, kept = partial_chunks(tokens, grad_out, slots[2:], rows)
    right = lax.ppermute(first, "fsdp", [(0, 1), (1, 2), (2, 3)])
    left = lax.ppermute(second, "fsdp", [(3, 2), (2, 1), (1, 0)])
    far_r = lax.ppermute(second, "fsdp", [(0, 1)])
    far_l = lax.ppermute(first, "fsdp", [(3, 2)])
    merged = (
        third.astype(jnp.float32)
        + jnp.where(f == 1, right.astype(jnp.float32), 0.0)
        + jnp.where(f == 2, left.astype(jnp.float32), 0.0)
    ).astype(bf16)
    two = lax.ppermute(merged, "fsdp", [(0, 2), (1, 3), (2, 0), (3, 1)])

    order = [(0, 0)]
    mask = 1
    while mask < n_f:
        held = jnp.concatenate([held, swap(held, "fsdp", n_f, mask)], axis=0)
        order = order + [(a, b ^ mask) for a, b in order]
        mask *= 2
    idx_near = held[:, :extra].astype(jnp.int32).reshape(n_f, 2, groups, LANES)
    mask = n_r // 2
    while mask >= 1:
        there = swap(held, "rep", n_r, mask)
        order = order + [(a ^ mask, b) for a, b in order]
        if mask > 1:
            held = jnp.concatenate([held, there], axis=0)
        mask //= 2
    idx_all = (
        jnp.concatenate([held[:, :extra], there[:, :extra]], axis=0)
        .astype(jnp.int32)
        .reshape(n_r, n_f, 2, groups, LANES)
    )
    order = np.array(order, np.int32)
    place = (jnp.asarray(order[:, 1]) ^ f) * n_r + (jnp.asarray(order[:, 0]) ^ r)

    values = select_values(me, inv, idx_near, tokens, grad_out, moment)
    mask = 1
    while mask < n_f:
        values = values + swap(values, "fsdp", n_f, mask)
        mask *= 2
    own_values = lax.dynamic_index_in_dim(values, f, 0, keepdims=False)
    sent = values.astype(bf16)[None]
    mask = n_r // 2
    while mask >= 1:
        sent = jnp.concatenate([sent, swap(sent, "rep", n_r, mask)], axis=0)
        mask //= 2

    base = moment_base(inv, idx_near, own_values, moment)
    old_out, coef = project(place.astype(jnp.int32), inv, next_tokens, held, there, extra)
    update, next_out = totals(me, inv, fwd, idx_all, sent.astype(jnp.float32), coef, old_out)

    near = jnp.where(f <= 1, left, right).astype(jnp.float32)
    grad = kept.astype(jnp.float32) + near + two.astype(jnp.float32) + far_r.astype(jnp.float32) + far_l.astype(jnp.float32)
    return update, (base + grad)[None], next_out


def cosine_table(order):
    return jnp.asarray(cosine_array(order), jnp.float32)


def forward_tiles(field, table):
    side = table.shape[0]
    shard_rows, width = field.shape
    tiles = field.reshape(shard_rows // side, side, width)
    along = jnp.einsum("ab,ibc->iac", table, tiles, precision=lax.Precision.HIGHEST)
    block = jnp.kron(jnp.eye(width // side, dtype=jnp.float32), table.T)
    return jnp.matmul(along, block, precision=lax.Precision.HIGHEST)


def inverse_tiles(spectra, table):
    side = table.shape[0]
    width = spectra.shape[2]
    along = jnp.einsum("ab,iac->ibc", table, spectra, precision=lax.Precision.HIGHEST)
    block = jnp.kron(jnp.eye(width // side, dtype=jnp.float32), table)
    result = jnp.matmul(along, block, precision=lax.Precision.HIGHEST)
    return result.reshape(spectra.shape[0] * side, width)


def one_hots(places, side, width):
    row_of = places // side
    col_of = places % side + jnp.arange(width // side, dtype=jnp.int32)[:, None] * side
    row_hot = (row_of[..., None] == jnp.arange(side, dtype=jnp.int32)).astype(jnp.float32)
    col_hot = (col_of[..., None] == jnp.arange(width, dtype=jnp.int32)).astype(jnp.float32)
    return (row_hot, col_hot)


def any_mesh(tokens, grad_out, moment, weight, next_tokens, index):
    table = cosine_table(TILE)
    width = weight.shape[1]
    partial = lax.dot_general(tokens, grad_out, (((0,), (0,)), ((), ())), preferred_element_type=jnp.float32)
    grad = lax.psum_scatter(partial.astype(jnp.bfloat16), "fsdp", scatter_dimension=0, tiled=True)
    moment_now = momentum_decay * moment[0] + grad.astype(jnp.float32)
    spectra = forward_tiles(moment_now, table)
    row_hot, col_hot = one_hots(index[0], TILE, width)
    picked = jnp.einsum("ijka,iac->ijkc", row_hot, spectra, precision=lax.Precision.HIGHEST)
    values = jnp.sum(picked * col_hot, axis=-1)
    dense = jnp.einsum("ijka,ijkc->iac", row_hot * values[..., None], col_hot, precision=lax.Precision.HIGHEST)
    new_moment = (moment_now - inverse_tiles(dense, table))[None]
    total = lax.psum(dense.astype(jnp.bfloat16), "rep").astype(jnp.float32)
    update = inverse_tiles(total, table)
    new_weight = (weight.astype(jnp.float32) - step_size * update).astype(jnp.bfloat16)
    full = lax.all_gather(new_weight, "fsdp", axis=0, tiled=True)
    next_out = jnp.dot(next_tokens, full, preferred_element_type=jnp.float32).astype(jnp.bfloat16)
    return (update, new_moment, next_out)


def solution(mesh):
    n_r, n_f = mesh.shape["rep"], mesh.shape["fsdp"]
    local = functools.partial(line_fast, n_r, n_f) if (n_r, n_f) == (8, 4) else any_mesh
    in_specs = (
        P(("rep", "fsdp"), None),
        P(("rep", "fsdp"), None),
        P("rep", "fsdp", None),
        P("fsdp", None),
        P(("rep", "fsdp"), None),
        P("rep", "fsdp", None, None),
    )
    out_specs = (P("fsdp", None), P("rep", "fsdp", None), P(("rep", "fsdp"), None))
    return jax.shard_map(local, mesh=mesh, in_specs=in_specs, out_specs=out_specs, check_vma=False)
```

```python
import functools

import jax
import jax.numpy as jnp
import numpy as np
from jax import lax
from jax.experimental import pallas as pl
from jax.experimental.pallas import tpu as pltpu
from jax.sharding import PartitionSpec as P

TILE = 64
LANES = 128

momentum_decay = 0.999
step_size = 0.005


def cosine_array(order):
    freq = np.arange(order, dtype=np.float64)[:, None]
    place = np.arange(order, dtype=np.float64)[None, :]
    table = np.sqrt(2.0 / order) * np.cos(np.pi * (2.0 * place + 1.0) * freq / (2.0 * order))
    return table * np.where(freq == 0.0, np.sqrt(0.5), 1.0)


def tables():
    block = np.kron(np.eye(2), cosine_array(TILE)).astype(np.float32)
    high = block.astype(jnp.bfloat16)
    low = (block - high.astype(np.float32)).astype(jnp.bfloat16)
    inv = np.concatenate([high.T, low.T], axis=0)
    fwd = np.concatenate([high, low], axis=0)
    return jnp.asarray(inv), jnp.asarray(fwd)


def split(x):
    high = x.astype(jnp.bfloat16)
    return high, (x - high.astype(jnp.float32)).astype(jnp.bfloat16)


def dot(a, b, contract=((1,), (0,))):
    return lax.dot_general(a, b, (contract, ((), ())), preferred_element_type=jnp.float32)


def hot(row, size, fill=None):
    spread = lambda x: jnp.broadcast_to(x, (16, LANES)).astype(jnp.bfloat16)
    place = spread(row)
    fill = jnp.ones((16, LANES), jnp.bfloat16) if fill is None else spread(fill)
    none = jnp.zeros((16, LANES), jnp.bfloat16)
    sub = lax.broadcasted_iota(jnp.int32, (16, LANES), 0).astype(jnp.float32)
    parts = [jnp.where((sub + 16.0 * i).astype(jnp.bfloat16) == place, fill, none) for i in range(size // 16)]
    return jnp.concatenate(parts, axis=0)


def partial_kernel(slots, tok, grad, *outs):
    for i, out in enumerate(outs):

        @pl.when(pl.program_id(0) == i)
        def _():
            out[...] = dot(tok[...], grad[...], ((0,), (0,))).astype(out.dtype)


def partial_chunks(tokens, grad_out, slots, rows):
    count = slots.shape[0]
    width = grad_out.shape[1]
    toks = tokens.shape[0]
    return pl.pallas_call(
        partial_kernel,
        grid_spec=pltpu.PrefetchScalarGridSpec(
            num_scalar_prefetch=1,
            grid=(count,),
            in_specs=[
                pl.BlockSpec((toks, rows), lambda s, slots: (0, slots[s])),
                pl.BlockSpec((toks, width), lambda s, slots: (0, 0)),
            ],
            out_specs=[pl.BlockSpec((rows, width), lambda s, slots: (0, 0)) for _ in range(count)],
        ),
        out_shape=[jax.ShapeDtypeStruct((rows, width), jnp.bfloat16) for _ in range(count)],
        cost_estimate=pl.CostEstimate(
            flops=2 * count * rows * width * toks, bytes_accessed=count * rows * (width + toks) * 2, transcendentals=0
        ),
        compiler_params=pltpu.CompilerParams(vmem_limit_bytes=32 * 2**20),
    )(slots, tokens, grad_out)


def entry_rows(inv, row, col):
    hots = jnp.concatenate([hot(row, LANES), hot(col, LANES)], axis=1)
    both = dot(inv, hots)
    return both[:LANES, :LANES], both[LANES:, :LANES], both[:LANES, LANES:], both[LANES:, LANES:]


def select_kernel(groups, me, inv_ref, idx_ref, tok_ref, grad_ref, moment_ref, out_ref):
    inv = inv_ref[...]
    grad = grad_ref[...]

    grad = jnp.concatenate([grad, grad], axis=1)
    places = idx_ref[0].astype(jnp.float32)

    def group(g, own):
        row = places[g : g + 1]
        col = places[groups + g : groups + g + 1]
        part = slice(g * LANES, (g + 1) * LANES)
        both = dot(inv, jnp.concatenate([hot(row, LANES), hot(col, LANES)], axis=1))
        a2 = both[:, :LANES].astype(jnp.bfloat16)
        b2 = both[:, LANES:].astype(jnp.bfloat16)
        tok = tok_ref[:, part]
        value = jnp.sum(dot(jnp.concatenate([tok, tok], axis=1), a2) * dot(grad, b2), axis=0, keepdims=True)
        if own:
            m_hi, m_lo = split(momentum_decay * moment_ref[part, :])
            mb = dot(jnp.concatenate([m_hi, m_hi], axis=1), b2) + dot(m_lo, b2[:LANES])
            value = value + jnp.sum(mb * (both[:LANES, :LANES] + both[LANES:, :LANES]), axis=0, keepdims=True)
        out_ref[0, g : g + 1, :] = value

    @pl.when(pl.program_id(0) == 0)
    def _():
        for g in range(groups):
            group(g, True)

    @pl.when(pl.program_id(0) != 0)
    def _():
        for g in range(groups):
            group(g, False)


def select_values(me, inv, idx, tokens, grad_out, moment):
    n_f = idx.shape[0]
    rows = moment.shape[0]
    groups = rows // LANES
    toks = tokens.shape[0]
    width = grad_out.shape[1]
    return pl.pallas_call(
        functools.partial(select_kernel, groups),
        grid_spec=pltpu.PrefetchScalarGridSpec(
            num_scalar_prefetch=1,
            grid=(n_f,),
            in_specs=[
                pl.BlockSpec(inv.shape, lambda s, me: (0, 0)),
                pl.BlockSpec((1, 2 * groups, LANES), lambda s, me: (s, 0, 0)),
                pl.BlockSpec((toks, rows), lambda s, me: (0, me[0] ^ s)),
                pl.BlockSpec((toks, width), lambda s, me: (0, 0)),
                pl.BlockSpec((rows, width), lambda s, me: (0, 0)),
            ],
            out_specs=pl.BlockSpec((1, groups, LANES), lambda s, me: (me[0] ^ s, 0, 0)),
        ),
        out_shape=jax.ShapeDtypeStruct((n_f, groups, LANES), jnp.float32),
        cost_estimate=pl.CostEstimate(
            flops=2 * n_f * groups * LANES**3 * 6, bytes_accessed=4 * 2**20, transcendentals=0
        ),
        compiler_params=pltpu.CompilerParams(vmem_limit_bytes=32 * 2**20),
    )(me, inv, idx, tokens, grad_out, moment)


def base_kernel(groups, me, inv_ref, idx_ref, val_ref, moment_ref, kept_ref, outer_ref, inner_ref, out_ref):
    inv = inv_ref[...]
    places = idx_ref[0].astype(jnp.float32)
    outer = (me[0] == 0) | (me[0] == me[1] - 1)
    for g in range(groups):
        a_hi, a_lo, b_hi, b_lo = entry_rows(inv, places[g : g + 1], places[groups + g : groups + g + 1])
        av_hi, av_lo = split((a_hi + a_lo) * val_ref[0, g : g + 1, :])
        left = jnp.concatenate([av_hi, av_hi, av_lo], axis=1)
        right = jnp.concatenate([b_hi, b_lo, b_hi], axis=1).astype(jnp.bfloat16)
        part = slice(g * LANES, (g + 1) * LANES)
        near = jnp.where(outer, outer_ref[part, :].astype(jnp.float32), inner_ref[part, :].astype(jnp.float32))
        got = kept_ref[part, :].astype(jnp.float32) + near
        out_ref[part, :] = (momentum_decay * moment_ref[part, :] + got) - dot(left, right, ((1,), (1,)))


def moment_base(me, inv, idx, values, moment, kept, outer, inner):
    groups = values.shape[1]
    rows, width = moment.shape
    slab = pl.BlockSpec((rows, width), lambda i, me: (0, 0))
    return pl.pallas_call(
        functools.partial(base_kernel, groups),
        grid_spec=pltpu.PrefetchScalarGridSpec(
            num_scalar_prefetch=1,
            grid=(1,),
            in_specs=[
                pl.BlockSpec(inv.shape, lambda i, me: (0, 0)),
                pl.BlockSpec((1, 2 * groups, LANES), lambda i, me: (0, 0, 0)),
                pl.BlockSpec((1, groups, LANES), lambda i, me: (me[0], 0, 0)),
                slab,
                slab,
                slab,
                slab,
            ],
            out_specs=slab,
        ),
        out_shape=jax.ShapeDtypeStruct((rows, width), jnp.float32),
        cost_estimate=pl.CostEstimate(
            flops=2 * groups * LANES**3 * 7, bytes_accessed=3 * rows * width * 4, transcendentals=0
        ),
        compiler_params=pltpu.CompilerParams(vmem_limit_bytes=32 * 2**20),
    )(me, inv, idx, values, moment, kept, outer, inner)


AWAY = (0, 4, 2, 6, 1, 5, 3, 7)


def project_kernel(n_r, n_f, extra, me, inv_ref, nt_ref, *refs):
    pieces, (out_ref, coef_ref) = refs[:n_r], refs[n_r:]
    width = nt_ref.shape[1]
    total = jnp.zeros(out_ref.shape, jnp.float32)
    size = width // (n_r * n_f)
    for away, piece in zip(AWAY, pieces):
        for p in range(n_f):
            place = (me[0] ^ p) * n_r + (me[2] ^ away)
            total += dot(nt_ref[:, pl.ds(pl.multiple_of(place * size, size), size)], piece[p, extra:, :])
    out_ref[...] = total
    inv = inv_ref[...]
    table = jnp.concatenate([inv[:LANES], inv[LANES:]], axis=1)
    for g in range(width // LANES):
        part = slice(g * LANES, (g + 1) * LANES)
        both = dot(nt_ref[:, part], table)
        coef_ref[:, part] = (both[:, :LANES] + both[:, LANES:]).astype(jnp.bfloat16)


def project(me, inv, next_tokens, pieces, extra):
    n_r, n_f = len(pieces), pieces[0].shape[0]
    toks, width = next_tokens.shape
    out = pieces[0].shape[2]
    full = lambda *shape: pl.BlockSpec(shape, lambda i, me: (0,) * len(shape))
    return pl.pallas_call(
        functools.partial(project_kernel, n_r, n_f, extra),
        grid_spec=pltpu.PrefetchScalarGridSpec(
            num_scalar_prefetch=1,
            grid=(1,),
            in_specs=[full(*inv.shape), full(toks, width)] + [full(*piece.shape) for piece in pieces],
            out_specs=[full(toks, out), full(toks, width)],
        ),
        out_shape=[jax.ShapeDtypeStruct((toks, out), jnp.float32), jax.ShapeDtypeStruct((toks, width), jnp.bfloat16)],
        cost_estimate=pl.CostEstimate(
            flops=2 * toks * width * out * 3, bytes_accessed=6 * toks * width * 2, transcendentals=0
        ),
        compiler_params=pltpu.CompilerParams(vmem_limit_bytes=48 * 2**20),
    )(me, inv, next_tokens, *pieces)


def total_kernel(groups, n_r, me, inv_ref, fwd_ref, coef_ref, base_ref, *refs):
    idx_refs, val_refs = refs[:n_r], refs[n_r : n_r + n_r // 2]
    up_ref, out_ref, acc_ref, sort_ref, dense_ref = refs[n_r + n_r // 2 :]
    step = pl.program_id(0)
    inv = inv_ref[...]
    fwd = fwd_ref[...]

    @pl.when(step == 0)
    def _():
        acc_ref[...] = jnp.zeros_like(acc_ref)

    lane = lax.broadcasted_iota(jnp.int32, (groups, LANES), 1)
    quarter = LANES // 4

    def regroup(parts):
        out = []
        for t in range(4):
            row = None
            for i, part in enumerate(parts):
                moved = part if i == t else pltpu.roll(part, (quarter * (i - t)) % LANES, 1)
                row = moved if row is None else jnp.where(lane // quarter == i, moved, row)
            out.append(row)
        return out

    for quad in range(n_r // 4):
        of = range(4 * quad, 4 * quad + 4)
        spots = [idx_refs[r][0].astype(jnp.int32) & (TILE - 1) for r in of]
        worth = [val_refs[r % (n_r // 2)][r // (n_r // 2), 0].astype(jnp.float32) for r in of]
        sets = regroup([x[:groups] for x in spots]), regroup([x[groups:] for x in spots]), regroup(worth)
        for kind, four in enumerate(sets):
            for t, rows in enumerate(four):
                sort_ref[kind, quad, t] = rows.astype(jnp.float32)

    def group(g):
        left, right = [], []
        for t in range(4):
            at = lambda kind, quad: sort_ref[kind, quad, t, pl.ds(g, 1), :]
            left.append(jnp.concatenate([hot(at(0, q), TILE) for q in range(n_r // 4)], axis=1))
            right.append(jnp.concatenate([hot(at(1, q), TILE, at(2, q)) for q in range(n_r // 4)], axis=1))
        cross = dot(jnp.concatenate(left, axis=0), jnp.concatenate(right, axis=0), ((1,), (1,)))
        low = lax.broadcasted_iota(jnp.int32, (TILE, LANES), 1) < TILE
        dense = jnp.concatenate(
            [
                jnp.where(low, cross[i : i + TILE, i : i + LANES], cross[i + TILE : i + LANES, i : i + LANES])
                for i in (0, LANES)
            ],
            axis=0,
        )
        q_hi, q_lo = split(dense)
        dense_ref[pl.ds(pl.multiple_of(g * LANES, LANES), LANES), :] = jnp.concatenate([q_hi, q_lo], axis=1)

    @pl.loop(0, groups, unroll=True)
    def _(g):
        group(g)

    both = dot(coef_ref[...], dense_ref[...])
    acc_ref[...] += both[:, :LANES] + both[:, LANES:]

    @pl.when(step == 0)
    def _():
        c_hi, c_lo = inv[:LANES], inv[LANES:]
        f_hi, f_lo = fwd[:LANES], fwd[LANES:]
        for g in range(groups):
            part = slice(g * LANES, (g + 1) * LANES)
            both = dot(jnp.concatenate([c_hi, c_lo], axis=1), jnp.concatenate([dense_ref[part, :], dense_ref[part, :]], axis=0))
            s_hi, s_lo = split(both[:, :LANES] + both[:, LANES:])
            up_ref[part, :] = dot(
                jnp.concatenate([s_hi, s_hi, s_lo], axis=1), jnp.concatenate([f_hi, f_lo, f_hi], axis=0)
            )

    @pl.when(step == pl.num_programs(0) - 1)
    def _():
        s_hi, s_lo = split(acc_ref[...])
        f_hi, f_lo = fwd[:LANES], fwd[LANES:]
        moved = dot(jnp.concatenate([s_hi, s_hi, s_lo], axis=1), jnp.concatenate([f_hi, f_lo, f_hi], axis=0))
        out_ref[...] = (base_ref[...] - step_size * moved).astype(out_ref.dtype)


def totals(me, inv, fwd, coef, base, pieces, sent):
    n_r, n_f = len(pieces), pieces[0].shape[0]
    groups = sent[0].shape[2]
    rows = groups * LANES
    toks, width = base.shape
    return pl.pallas_call(
        functools.partial(total_kernel, groups, n_r),
        grid_spec=pltpu.PrefetchScalarGridSpec(
            num_scalar_prefetch=1,
            grid=(n_f,),
            in_specs=[
                pl.BlockSpec(inv.shape, lambda s, me: (0, 0)),
                pl.BlockSpec(fwd.shape, lambda s, me: (0, 0)),
                pl.BlockSpec((toks, rows), lambda s, me: (0, me[0] ^ s)),
                pl.BlockSpec((toks, width), lambda s, me: (0, 0)),
            ]
            + [pl.BlockSpec((1, 2 * groups, LANES), lambda s, me: (s, 0, 0)) for _ in pieces]
            + [pl.BlockSpec((2, 1, groups, LANES), lambda s, me: (0, me[0] ^ s, 0, 0)) for _ in sent],
            out_specs=[
                pl.BlockSpec((rows, width), lambda s, me: (0, 0)),
                pl.BlockSpec((toks, width), lambda s, me: (0, 0)),
            ],
            scratch_shapes=[
                pltpu.VMEM((toks, width), jnp.float32),
                pltpu.VMEM((3, n_r // 4, 4, groups, LANES), jnp.float32),
                pltpu.VMEM((rows, 2 * LANES), jnp.bfloat16),
            ],
        ),
        out_shape=[
            jax.ShapeDtypeStruct((rows, width), jnp.float32),
            jax.ShapeDtypeStruct((toks, width), jnp.bfloat16),
        ],
        cost_estimate=pl.CostEstimate(
            flops=2 * n_f * groups * LANES**3 * (n_r + 2), bytes_accessed=4 * 2**20, transcendentals=0
        ),
        compiler_params=pltpu.CompilerParams(vmem_limit_bytes=32 * 2**20),
    )(me, inv, fwd, coef, base, *pieces, *sent)


def swap(x, axis, size, mask):
    return lax.ppermute(x, axis, [(i, i ^ mask) for i in range(size)])


def fence(stage, *args):
    shapes = jax.eval_shape(stage, *args)
    other = lambda *args: jax.tree.map(lambda x: jnp.zeros(x.shape, x.dtype), shapes)
    return lax.cond(lax.axis_index("rep") < lax.axis_size("rep"), stage, other, *args)


SLOTS = np.array([[3, 1, 2, 0], [0, 2, 3, 1], [3, 1, 0, 2], [0, 2, 1, 3]], np.int32)


def line_fast(n_r, n_f, tokens, grad_out, moment, weight, next_tokens, index):
    bf16 = jnp.bfloat16
    r, f = lax.axis_index("rep"), lax.axis_index("fsdp")
    me = jnp.stack([f, n_f, r]).astype(jnp.int32)
    inv, fwd = tables()
    moment = moment[0]
    rows = moment.shape[0]
    groups = rows // LANES
    slice_rows = rows // n_r

    flat = index[0].reshape(groups, LANES)
    lane = jnp.arange(LANES, dtype=jnp.int32)
    row_pos = flat // TILE + (lane // TILE) * TILE
    col_pos = flat % TILE + (lane // (TILE // 2)) % 2 * TILE
    own_idx = jnp.concatenate([row_pos, col_pos], axis=0).astype(bf16)
    extra = own_idx.shape[0]
    share = lax.dynamic_slice_in_dim(weight, r * slice_rows, slice_rows, axis=0)
    held = jnp.concatenate([own_idx, share], axis=0)[None]

    held = jnp.concatenate([held] + [swap(held, "fsdp", n_f, p) for p in range(1, n_f)], axis=0)
    slots = jnp.asarray(SLOTS)[f]
    first, second, third, kept = partial_chunks(tokens, grad_out, slots, rows)
    held, first, second = lax.optimization_barrier((held, first, second))
    outer = lax.ppermute(first, "fsdp", [(0, 1), (1, 0), (2, 3), (3, 2)])
    inner = lax.ppermute(second, "fsdp", [(1, 2), (2, 1)])

    def near_stage(held):
        pieces = [swap(held, "rep", n_r, away) for away in AWAY[1 : n_r // 2]]
        return select_values(me, inv, held, tokens, grad_out, moment), pieces

    values, pieces = fence(near_stage, held)
    pieces = [held] + pieces

    outer, inner = lax.optimization_barrier((outer, inner))

    def sum_stage(values, third, outer, pieces):
        parts = [swap(values, "fsdp", n_f, p) for p in range(1, n_f)]
        more = [swap(piece, "rep", n_r, 1) for piece in pieces]
        got = jnp.where((f == 1) | (f == 2), outer.astype(jnp.float32), 0.0)
        merged = (third.astype(jnp.float32) + got).astype(bf16)
        return sum(parts, values), more, merged

    values, more, merged = fence(sum_stage, values, third, outer, pieces)
    values, merged, second = lax.optimization_barrier((values, merged, second))
    two = lax.ppermute(merged, "fsdp", [(0, 2), (1, 3), (2, 0), (3, 1)])
    far = lax.ppermute(second, "fsdp", [(0, 1), (3, 2)])

    def far_stage(values, pieces, kept, outer, inner):
        sent = values.astype(bf16)[None]
        sent = jnp.concatenate([sent, swap(sent, "rep", n_r, 1)], axis=0)
        sents = [sent] + [swap(sent, "rep", n_r, away) for away in AWAY[1 : n_r // 2]]
        base = moment_base(me, inv, held, values, moment, kept, outer, inner)
        old_out, coef = project(me, inv, next_tokens, pieces, extra)
        return sents, base, old_out, coef

    pieces = pieces + more
    sents, base, old_out, coef = fence(far_stage, values, pieces, kept, outer, inner)
    update, next_out = totals(me, inv, fwd, coef, old_out, pieces, sents)
    grad = two.astype(jnp.float32) + far.astype(jnp.float32)
    return update, (base + grad)[None], next_out


def cosine_table(order):
    return jnp.asarray(cosine_array(order), jnp.float32)


def forward_tiles(field, table):
    side = table.shape[0]
    shard_rows, width = field.shape
    tiles = field.reshape(shard_rows // side, side, width)
    along = jnp.einsum("ab,ibc->iac", table, tiles, precision=lax.Precision.HIGHEST)
    block = jnp.kron(jnp.eye(width // side, dtype=jnp.float32), table.T)
    return jnp.matmul(along, block, precision=lax.Precision.HIGHEST)


def inverse_tiles(spectra, table):
    side = table.shape[0]
    width = spectra.shape[2]
    along = jnp.einsum("ab,iac->ibc", table, spectra, precision=lax.Precision.HIGHEST)
    block = jnp.kron(jnp.eye(width // side, dtype=jnp.float32), table)
    result = jnp.matmul(along, block, precision=lax.Precision.HIGHEST)
    return result.reshape(spectra.shape[0] * side, width)


def one_hots(places, side, width):
    row_of = places // side
    col_of = places % side + jnp.arange(width // side, dtype=jnp.int32)[:, None] * side
    row_hot = (row_of[..., None] == jnp.arange(side, dtype=jnp.int32)).astype(jnp.float32)
    col_hot = (col_of[..., None] == jnp.arange(width, dtype=jnp.int32)).astype(jnp.float32)
    return (row_hot, col_hot)


def any_mesh(tokens, grad_out, moment, weight, next_tokens, index):
    table = cosine_table(TILE)
    width = weight.shape[1]
    partial = lax.dot_general(tokens, grad_out, (((0,), (0,)), ((), ())), preferred_element_type=jnp.float32)
    grad = lax.psum_scatter(partial.astype(jnp.bfloat16), "fsdp", scatter_dimension=0, tiled=True)
    moment_now = momentum_decay * moment[0] + grad.astype(jnp.float32)
    spectra = forward_tiles(moment_now, table)
    row_hot, col_hot = one_hots(index[0], TILE, width)
    picked = jnp.einsum("ijka,iac->ijkc", row_hot, spectra, precision=lax.Precision.HIGHEST)
    values = jnp.sum(picked * col_hot, axis=-1)
    dense = jnp.einsum("ijka,ijkc->iac", row_hot * values[..., None], col_hot, precision=lax.Precision.HIGHEST)
    new_moment = (moment_now - inverse_tiles(dense, table))[None]
    total = lax.psum(dense.astype(jnp.bfloat16), "rep").astype(jnp.float32)
    update = inverse_tiles(total, table)
    new_weight = (weight.astype(jnp.float32) - step_size * update).astype(jnp.bfloat16)
    full = lax.all_gather(new_weight, "fsdp", axis=0, tiled=True)
    next_out = jnp.dot(next_tokens, full, preferred_element_type=jnp.float32).astype(jnp.bfloat16)
    return (update, new_moment, next_out)


def solution(mesh):
    n_r, n_f = mesh.shape["rep"], mesh.shape["fsdp"]
    local = functools.partial(line_fast, n_r, n_f) if (n_r, n_f) == (8, 4) else any_mesh
    in_specs = (
        P(("rep", "fsdp"), None),
        P(("rep", "fsdp"), None),
        P("rep", "fsdp", None),
        P("fsdp", None),
        P(("rep", "fsdp"), None),
        P("rep", "fsdp", None, None),
    )
    out_specs = (P("fsdp", None), P("rep", "fsdp", None), P(("rep", "fsdp"), None))
    return jax.shard_map(local, mesh=mesh, in_specs=in_specs, out_specs=out_specs, check_vma=False)
```

```python
import functools

import jax
import jax.numpy as jnp
import numpy as np
from jax import lax
from jax.experimental import pallas as pl
from jax.experimental.pallas import tpu as pltpu
from jax.sharding import PartitionSpec as P

TILE = 64
LANES = 128

momentum_decay = 0.999
step_size = 0.005


def cosine_array(order):
    freq = np.arange(order, dtype=np.float64)[:, None]
    place = np.arange(order, dtype=np.float64)[None, :]
    table = np.sqrt(2.0 / order) * np.cos(np.pi * (2.0 * place + 1.0) * freq / (2.0 * order))
    return table * np.where(freq == 0.0, np.sqrt(0.5), 1.0)


def tables():
    block = np.kron(np.eye(2), cosine_array(TILE)).astype(np.float32)
    high = block.astype(jnp.bfloat16)
    low = (block - high.astype(np.float32)).astype(jnp.bfloat16)
    inv = np.concatenate([high.T, low.T], axis=0)
    small = [part[i : i + TILE, i : i + TILE].T for i in (0, TILE) for part in (high, low)]
    pair = np.zeros((4 * TILE, LANES), jnp.bfloat16)
    for i, part in enumerate(small):
        pair[i * TILE : (i + 1) * TILE, (i // 2) * TILE : (i // 2 + 1) * TILE] = part
    fwd = np.concatenate([high, low], axis=0)
    return jnp.asarray(inv), jnp.asarray(fwd), jnp.asarray(pair)


def split(x):
    high = x.astype(jnp.bfloat16)
    return high, (x - high.astype(jnp.float32)).astype(jnp.bfloat16)


def dot(a, b, contract=((1,), (0,))):
    return lax.dot_general(a, b, (contract, ((), ())), preferred_element_type=jnp.float32)


def hot(row, size, fill=None):
    spread = lambda x: jnp.broadcast_to(x, (16, LANES)).astype(jnp.bfloat16)
    place = spread(row)
    fill = jnp.ones((16, LANES), jnp.bfloat16) if fill is None else spread(fill)
    none = jnp.zeros((16, LANES), jnp.bfloat16)
    sub = lax.broadcasted_iota(jnp.int32, (16, LANES), 0).astype(jnp.float32)
    parts = [jnp.where((sub + 16.0 * i).astype(jnp.bfloat16) == place, fill, none) for i in range(size // 16)]
    return jnp.concatenate(parts, axis=0)


def chunk_of(slot, f):
    return jnp.where(slot < 2, jnp.where(slot == 0, 3 - 3 * (f & 1), 1 + (f & 1)), jnp.where(slot == 2, f ^ 2, f))


def partial_kernel(me, tok, grad, *outs):
    for i, out in enumerate(outs):

        @pl.when(pl.program_id(0) == i)
        def _():
            out[...] = dot(tok[...], grad[...], ((0,), (0,))).astype(out.dtype)


def partial_chunks(me, tokens, grad_out, rows):
    count = 4
    width = grad_out.shape[1]
    toks = tokens.shape[0]
    return pl.pallas_call(
        partial_kernel,
        grid_spec=pltpu.PrefetchScalarGridSpec(
            num_scalar_prefetch=1,
            grid=(count,),
            in_specs=[
                pl.BlockSpec((toks, rows), lambda s, me: (0, chunk_of(s, me[0]))),
                pl.BlockSpec((toks, width), lambda s, me: (0, 0)),
            ],
            out_specs=[pl.BlockSpec((rows, width), lambda s, me: (0, 0)) for _ in range(count)],
        ),
        out_shape=[jax.ShapeDtypeStruct((rows, width), jnp.bfloat16) for _ in range(count)],
        cost_estimate=pl.CostEstimate(
            flops=2 * count * rows * width * toks, bytes_accessed=count * rows * (width + toks) * 2, transcendentals=0
        ),
        compiler_params=pltpu.CompilerParams(vmem_limit_bytes=32 * 2**20),
    )(me, tokens, grad_out)


def idx_block(s, unit):
    return jnp.where(s == 0, 0, unit * (s - 1) + 1)


def select_kernel(groups, me, pair_ref, idx_ref, tok_ref, grad_ref, moment_ref, out_ref):
    pair = pair_ref[...]
    grad = jnp.concatenate([grad_ref[...]] * 2, axis=1)
    places = (idx_ref[...].astype(jnp.int32) & (TILE - 1)).astype(jnp.float32)
    lane = lax.broadcasted_iota(jnp.int32, (TILE, LANES), 1)
    top = lane < TILE
    even = (lane // (TILE // 2)) % 2 == 0
    none = jnp.zeros((TILE, LANES), jnp.float32)

    def spread(low_half, high, low):
        parts = [jnp.where(low_half, high, none), jnp.where(low_half, none, high)]
        parts += [jnp.where(low_half, low, none), jnp.where(low_half, none, low)]
        return jnp.concatenate(parts, axis=0)

    batch = groups

    def some_groups(g, own):
        of = range(g, g + batch)
        rows = [jnp.concatenate([hot(places[i : i + 1], TILE), hot(places[groups + i : groups + i + 1], TILE)], axis=0) for i in of]
        both = dot(pair, jnp.concatenate(rows, axis=1))
        quarters = [[both[q * TILE : (q + 1) * TILE, i * LANES : (i + 1) * LANES] for q in range(4)] for i in range(batch)]
        a2s = [spread(top, quarter[0], quarter[1]) for quarter in quarters]
        b2s = [spread(even, quarter[2], quarter[3]).astype(jnp.bfloat16) for quarter in quarters]
        gb = dot(grad, jnp.concatenate(b2s, axis=1))
        toks = [tok_ref[:, i * LANES : (i + 1) * LANES] for i in of]
        tas = [dot(jnp.concatenate([tok, tok], axis=1), a2.astype(jnp.bfloat16)) for tok, a2 in zip(toks, a2s)]
        values = [
            jnp.sum(ta * gb[:, i * LANES : (i + 1) * LANES], axis=0, keepdims=True) for i, ta in enumerate(tas)
        ]
        if own:
            parts = [split(momentum_decay * moment_ref[i * LANES : (i + 1) * LANES, :]) for i in of]
            mbs = [
                dot(jnp.concatenate([hi, hi], axis=1), b2) + dot(lo, b2[:LANES]) for (hi, lo), b2 in zip(parts, b2s)
            ]
            values = [
                value + jnp.sum(mb * (a2[:LANES] + a2[LANES:]), axis=0, keepdims=True)
                for value, mb, a2 in zip(values, mbs, a2s)
            ]
        out_ref[0, g : g + batch, :] = jnp.concatenate(values, axis=0)

    @pl.when(pl.program_id(0) == 0)
    def _():
        for g in range(0, groups, batch):
            some_groups(g, True)

    @pl.when(pl.program_id(0) != 0)
    def _():
        for g in range(0, groups, batch):
            some_groups(g, False)


def select_values(me, inv, idx, unit, tokens, grad_out, moment):
    n_f = tokens.shape[1] // moment.shape[0]
    rows = moment.shape[0]
    groups = rows // LANES
    toks = tokens.shape[0]
    width = grad_out.shape[1]
    return pl.pallas_call(
        functools.partial(select_kernel, groups),
        grid_spec=pltpu.PrefetchScalarGridSpec(
            num_scalar_prefetch=1,
            grid=(n_f,),
            in_specs=[
                pl.BlockSpec(inv.shape, lambda s, me: (0, 0)),
                pl.BlockSpec((2 * groups, LANES), lambda s, me: (idx_block(s, unit), 0)),
                pl.BlockSpec((toks, rows), lambda s, me: (0, me[0] ^ s)),
                pl.BlockSpec((toks, width), lambda s, me: (0, 0)),
                pl.BlockSpec((rows, width), lambda s, me: (0, 0)),
            ],
            out_specs=pl.BlockSpec((1, groups, LANES), lambda s, me: (me[0] ^ s, 0, 0)),
        ),
        out_shape=jax.ShapeDtypeStruct((n_f, groups, LANES), jnp.float32),
        cost_estimate=pl.CostEstimate(
            flops=2 * n_f * groups * LANES**3 * 6, bytes_accessed=4 * 2**20, transcendentals=0
        ),
        compiler_params=pltpu.CompilerParams(vmem_limit_bytes=32 * 2**20),
    )(me, inv, idx, tokens, grad_out, moment)


def moment_kernel(groups, me, inv_ref, idx_ref, val_ref, moment_ref, kept_ref, outer_ref, inner_ref, two_ref, far_ref, out_ref):
    inv = inv_ref[...]
    outer = (me[0] == 0) | (me[0] == me[1] - 1)
    step = groups // 2
    first = pl.multiple_of(pl.program_id(0) * step, step)
    row_at = idx_ref[...].astype(jnp.float32)
    upper = pl.program_id(0) > 0
    pick = lambda x: jnp.where(upper, x[step:], x[:step])
    rows, cols, worth = pick(row_at[:groups]), pick(row_at[groups:]), pick(val_ref[0])
    of = range(step)
    hots = [jnp.concatenate([hot(rows[g : g + 1], LANES), hot(cols[g : g + 1], LANES)], axis=1) for g in of]
    both = dot(inv, jnp.concatenate(hots, axis=1))
    block = lambda half, g: both[half * LANES : (half + 1) * LANES, g * LANES : (g + 1) * LANES]
    lefts = [split((block(0, 2 * g) + block(1, 2 * g)) * worth[g : g + 1, :]) for g in of]
    lefts = [jnp.concatenate([hi, hi, lo], axis=1) for hi, lo in lefts]
    rights = [jnp.concatenate([block(0, 2 * g + 1), block(1, 2 * g + 1)], axis=1).astype(jnp.bfloat16) for g in of]
    rights = [jnp.concatenate([right, right[:, :LANES]], axis=1) for right in rights]
    slabs = jnp.concatenate([dot(left, right, ((1,), (1,))) for left, right in zip(lefts, rights)], axis=0)
    wide = lambda ref: ref[...].astype(jnp.float32)
    got = wide(kept_ref) + jnp.where(outer, wide(outer_ref), wide(inner_ref)) + (wide(two_ref) + wide(far_ref))
    out_ref[...] = (momentum_decay * moment_ref[...] + got) - slabs


def new_moment_of(me, inv, idx, values, moment, *parts):
    groups = values.shape[1]
    rows, width = moment.shape
    slab = pl.BlockSpec((rows // 2, width), lambda i, me: (i, 0))
    return pl.pallas_call(
        functools.partial(moment_kernel, groups),
        grid_spec=pltpu.PrefetchScalarGridSpec(
            num_scalar_prefetch=1,
            grid=(2,),
            in_specs=[
                pl.BlockSpec(inv.shape, lambda i, me: (0, 0)),
                pl.BlockSpec((2 * groups, LANES), lambda i, me: (0, 0)),
                pl.BlockSpec((1, groups, LANES), lambda i, me: (me[0], 0, 0)),
                slab,
            ]
            + [slab for _ in parts],
            out_specs=slab,
        ),
        out_shape=jax.ShapeDtypeStruct((rows, width), jnp.float32),
        cost_estimate=pl.CostEstimate(
            flops=2 * groups * LANES**3 * 7, bytes_accessed=5 * rows * width * 4, transcendentals=0
        ),
        compiler_params=pltpu.CompilerParams(vmem_limit_bytes=32 * 2**20),
    )(me, inv, idx, values, moment, *parts)


AWAY = (0, 4, 2, 6, 1, 5, 3, 7)


def project_kernel(n_r, n_f, extra, me, inv_ref, nt_ref, weight_ref, *refs):
    pieces, (out_ref, coef_ref) = refs[:n_r], refs[n_r:]
    width = nt_ref.shape[1]
    size = width // (n_r * n_f)
    near = nt_ref[:, pl.ds(pl.multiple_of(me[0] * size * n_r, size * n_r), size * n_r)]
    total = dot(near, weight_ref[...])
    for p in range(1, n_f):
        lefts, rights = [], []
        for away, piece in zip(AWAY, pieces):
            place = (me[0] ^ p) * n_r + (me[2] ^ away)
            lefts.append(nt_ref[:, pl.ds(pl.multiple_of(place * size, size), size)])
            rights.append(piece[p * (extra + size) - size + extra : p * (extra + size) + extra, :])
        total += dot(jnp.concatenate(lefts, axis=1), jnp.concatenate(rights, axis=0))
    out_ref[...] = total
    inv = inv_ref[...]
    table = jnp.concatenate([inv[:LANES], inv[LANES:]], axis=1)
    toks = nt_ref.shape[0]
    batch = 8
    for g in range(0, width // LANES, batch):
        parts = [slice(i * LANES, (i + 1) * LANES) for i in range(g, g + batch)]
        both = dot(jnp.concatenate([nt_ref[:, part] for part in parts], axis=0), table)
        both = (both[:, :LANES] + both[:, LANES:]).astype(jnp.bfloat16)
        for i, part in enumerate(parts):
            coef_ref[:, part] = both[i * toks : (i + 1) * toks]


def project(me, inv, next_tokens, weight, pieces, extra):
    n_r = len(pieces)
    toks, width = next_tokens.shape
    n_f = width // weight.shape[0]
    out = weight.shape[1]
    full = lambda *shape: pl.BlockSpec(shape, lambda i, me: (0,) * len(shape))
    return pl.pallas_call(
        functools.partial(project_kernel, n_r, n_f, extra),
        grid_spec=pltpu.PrefetchScalarGridSpec(
            num_scalar_prefetch=1,
            grid=(1,),
            in_specs=[full(*inv.shape), full(toks, width), full(*weight.shape)] + [full(*piece.shape) for piece in pieces],
            out_specs=[full(toks, out), full(toks, width)],
        ),
        out_shape=[jax.ShapeDtypeStruct((toks, out), jnp.float32), jax.ShapeDtypeStruct((toks, width), jnp.bfloat16)],
        cost_estimate=pl.CostEstimate(
            flops=2 * toks * width * out * 3, bytes_accessed=6 * toks * width * 2, transcendentals=0
        ),
        compiler_params=pltpu.CompilerParams(vmem_limit_bytes=48 * 2**20),
    )(me, inv, next_tokens, weight, *pieces)


def merge_kernel(me, third_ref, outer_ref, out_ref):
    inner = (me[0] > 0) & (me[0] < me[1] - 1)

    @pl.when(inner)
    def _():
        out_ref[...] = (third_ref[...].astype(jnp.float32) + outer_ref[...].astype(jnp.float32)).astype(out_ref.dtype)

    @pl.when(jnp.logical_not(inner))
    def _():
        out_ref[...] = third_ref[...]


def merge(me, third, outer):
    rows, width = third.shape
    slab = pl.BlockSpec((rows // 4, width), lambda i, me: (i, 0))
    return pl.pallas_call(
        merge_kernel,
        grid_spec=pltpu.PrefetchScalarGridSpec(num_scalar_prefetch=1, grid=(4,), in_specs=[slab, slab], out_specs=slab),
        out_shape=jax.ShapeDtypeStruct((rows, width), third.dtype),
        cost_estimate=pl.CostEstimate(flops=rows * width, bytes_accessed=6 * rows * width, transcendentals=0),
    )(me, third, outer)


def total_kernel(groups, n_r, me, inv_ref, fwd_ref, coef_ref, base_ref, *refs):
    idx_refs, val_refs = refs[:n_r], refs[n_r : n_r + n_r // 2]
    up_ref, out_ref, acc_ref, sort_ref, dense_ref = refs[n_r + n_r // 2 :]
    step = pl.program_id(0)
    inv = inv_ref[...]
    fwd = fwd_ref[...]

    @pl.when(step == 0)
    def _():
        acc_ref[...] = jnp.zeros_like(acc_ref)

    lane = lax.broadcasted_iota(jnp.int32, (groups, LANES), 1)
    quarter = LANES // 4

    def regroup(parts):
        out = []
        for t in range(4):
            row = None
            for i, part in enumerate(parts):
                moved = part if i == t else pltpu.roll(part, (quarter * (i - t)) % LANES, 1)
                row = moved if row is None else jnp.where(lane // quarter == i, moved, row)
            out.append(row)
        return out

    for quad in range(n_r // 4):
        of = range(4 * quad, 4 * quad + 4)
        spots = [idx_refs[r][...].astype(jnp.int32) & (TILE - 1) for r in of]
        worth = [val_refs[r % (n_r // 2)][r // (n_r // 2), 0].astype(jnp.float32) for r in of]
        sets = regroup([x[:groups] for x in spots]), regroup([x[groups:] for x in spots]), regroup(worth)
        for kind, four in enumerate(sets):
            for t, rows in enumerate(four):
                sort_ref[kind, quad, t] = rows.astype(jnp.float32)

    low = lax.broadcasted_iota(jnp.int32, (TILE, LANES), 1) < TILE
    batch = 2

    def some_groups(g):
        of = range(g, g + batch)
        at = lambda kind, quad, t, i: sort_ref[kind, quad, t, i : i + 1, :]
        quads = range(n_r // 4)
        side = lambda tile: jnp.concatenate([jnp.concatenate([tile(t, q) for q in quads], axis=1) for t in range(4)], axis=0)
        lefts = [side(lambda t, q: hot(at(0, q, t, i), TILE)) for i in of]
        rights = [side(lambda t, q: hot(at(1, q, t, i), TILE, at(2, q, t, i))) for i in of]
        crosses = [dot(left, right, ((1,), (1,))) for left, right in zip(lefts, rights)]
        diagonal = lambda cross, i: jnp.where(low, cross[i : i + TILE, i : i + LANES], cross[i + TILE : i + LANES, i : i + LANES])
        denses = [jnp.concatenate([diagonal(cross, 0), diagonal(cross, LANES)], axis=0) for cross in crosses]
        for i, dense in zip(of, denses):
            dense_ref[i * LANES : (i + 1) * LANES, :] = jnp.concatenate(split(dense), axis=1)

    for g in range(0, groups, batch):
        some_groups(g)

    both = dot(coef_ref[...], dense_ref[...])
    acc_ref[...] += both[:, :LANES] + both[:, LANES:]

    @pl.when(step == 0)
    def _():
        c_hi, c_lo = inv[:LANES], inv[LANES:]
        f_hi, f_lo = fwd[:LANES], fwd[LANES:]
        table = jnp.concatenate([c_hi, c_lo], axis=1)
        last = jnp.concatenate([f_hi, f_lo, f_hi], axis=0)
        parts = [dense_ref[g * LANES : (g + 1) * LANES, :] for g in range(groups)]
        boths = [dot(table, jnp.concatenate([part, part], axis=0)) for part in parts]
        halves = [split(both[:, :LANES] + both[:, LANES:]) for both in boths]
        lines = jnp.concatenate([jnp.concatenate([hi, hi, lo], axis=1) for hi, lo in halves], axis=0)
        up_ref[...] = dot(lines, last)

    @pl.when(step == pl.num_programs(0) - 1)
    def _():
        s_hi, s_lo = split(acc_ref[...])
        f_hi, f_lo = fwd[:LANES], fwd[LANES:]
        moved = dot(jnp.concatenate([s_hi, s_hi, s_lo], axis=1), jnp.concatenate([f_hi, f_lo, f_hi], axis=0))
        out_ref[...] = (base_ref[...] - step_size * moved).astype(out_ref.dtype)


def totals(me, inv, fwd, coef, base, pieces, unit, sent):
    n_r, n_f = len(pieces), sent[0].shape[1]
    groups = sent[0].shape[2]
    rows = groups * LANES
    toks, width = base.shape
    return pl.pallas_call(
        functools.partial(total_kernel, groups, n_r),
        grid_spec=pltpu.PrefetchScalarGridSpec(
            num_scalar_prefetch=1,
            grid=(n_f,),
            in_specs=[
                pl.BlockSpec(inv.shape, lambda s, me: (0, 0)),
                pl.BlockSpec(fwd.shape, lambda s, me: (0, 0)),
                pl.BlockSpec((toks, rows), lambda s, me: (0, me[0] ^ s)),
                pl.BlockSpec((toks, width), lambda s, me: (0, 0)),
            ]
            + [pl.BlockSpec((2 * groups, LANES), lambda s, me: (idx_block(s, unit), 0)) for _ in pieces]
            + [pl.BlockSpec((2, 1, groups, LANES), lambda s, me: (0, me[0] ^ s, 0, 0)) for _ in sent],
            out_specs=[
                pl.BlockSpec((rows, width), lambda s, me: (0, 0)),
                pl.BlockSpec((toks, width), lambda s, me: (0, 0)),
            ],
            scratch_shapes=[
                pltpu.VMEM((toks, width), jnp.float32),
                pltpu.VMEM((3, n_r // 4, 4, groups, LANES), jnp.float32),
                pltpu.VMEM((rows, 2 * LANES), jnp.bfloat16),
            ],
        ),
        out_shape=[
            jax.ShapeDtypeStruct((rows, width), jnp.float32),
            jax.ShapeDtypeStruct((toks, width), jnp.bfloat16),
        ],
        cost_estimate=pl.CostEstimate(
            flops=2 * n_f * groups * LANES**3 * (n_r + 2), bytes_accessed=4 * 2**20, transcendentals=0
        ),
        compiler_params=pltpu.CompilerParams(vmem_limit_bytes=32 * 2**20),
    )(me, inv, fwd, coef, base, *pieces, *sent)


def swap(x, axis, size, mask):
    return lax.ppermute(x, axis, [(i, i ^ mask) for i in range(size)])


def fence(stage, *args):
    shapes = jax.eval_shape(stage, *args)
    other = lambda *args: jax.tree.map(lambda x: jnp.zeros(x.shape, x.dtype), shapes)
    return lax.cond(lax.axis_index("rep") < lax.axis_size("rep"), stage, other, *args)


def line_fast(n_r, n_f, tokens, grad_out, moment, weight, next_tokens, index):
    bf16 = jnp.bfloat16
    r, f = lax.axis_index("rep"), lax.axis_index("fsdp")
    me = jnp.stack([f, n_f, r]).astype(jnp.int32)
    inv, fwd, pair = tables()
    moment = moment[0]
    rows = moment.shape[0]
    groups = rows // LANES
    slice_rows = rows // n_r

    flat = index[0].reshape(groups, LANES)
    lane = jnp.arange(LANES, dtype=jnp.int32)
    row_pos = flat // TILE + (lane // TILE) * TILE
    col_pos = flat % TILE + (lane // (TILE // 2)) % 2 * TILE
    own_idx = jnp.concatenate([row_pos, col_pos], axis=0).astype(bf16)
    extra = own_idx.shape[0]
    share = lax.dynamic_slice_in_dim(weight, r * slice_rows, slice_rows, axis=0)
    held = jnp.concatenate([own_idx, share], axis=0)
    unit = held.shape[0] // extra

    held = jnp.concatenate([own_idx] + [swap(held, "fsdp", n_f, p) for p in range(1, n_f)], axis=0)
    first, second, third, kept = partial_chunks(me, tokens, grad_out, rows)
    held, first, second = lax.optimization_barrier((held, first, second))
    outer = lax.ppermute(first, "fsdp", [(0, 1), (1, 0), (2, 3), (3, 2)])
    inner = lax.ppermute(second, "fsdp", [(1, 2), (2, 1)])

    def near_stage(held):
        pieces = [swap(held, "rep", n_r, away) for away in AWAY[1 : n_r // 2]]
        return select_values(me, pair, held, unit, tokens, grad_out, moment), pieces

    values, pieces = fence(near_stage, held)
    pieces = [held] + pieces
    outer, inner = lax.optimization_barrier((outer, inner))

    def sum_stage(values, third, outer, pieces):
        parts = [swap(values, "fsdp", n_f, p) for p in range(1, n_f)]
        more = [swap(piece, "rep", n_r, 1) for piece in pieces]
        return parts, merge(me, third, outer), more

    parts, merged, more = fence(sum_stage, values, third, outer, pieces[:2])
    parts, merged, second = lax.optimization_barrier((parts, merged, second))
    two = lax.ppermute(merged, "fsdp", [(0, 2), (1, 3), (2, 0), (3, 1)])
    far = lax.ppermute(second, "fsdp", [(0, 1), (3, 2)])

    def far_stage(values, parts, pieces, more):
        summed = sum(parts, values)
        sent = summed.astype(bf16)[None]
        last = [swap(piece, "rep", n_r, 1) for piece in pieces[2:]]
        sent = jnp.concatenate([sent, swap(sent, "rep", n_r, 1)], axis=0)
        sent, last = lax.optimization_barrier((sent, last))
        sents = [sent] + [swap(sent, "rep", n_r, away) for away in AWAY[1 : n_r // 2]]
        old_out, coef = project(me, inv, next_tokens, weight, pieces + more + last, extra)
        return summed, sents, old_out, coef, last

    values, sents, old_out, coef, last = fence(far_stage, values, parts, pieces, more)
    pieces = pieces + more + last
    update, next_out = totals(me, inv, fwd, coef, old_out, pieces, unit, sents)
    update, two, far = lax.optimization_barrier((update, two, far))
    new_moment = new_moment_of(me, inv, held, values, moment, kept, outer, inner, two, far)
    return update, new_moment[None], next_out


def cosine_table(order):
    return jnp.asarray(cosine_array(order), jnp.float32)


def forward_tiles(field, table):
    side = table.shape[0]
    shard_rows, width = field.shape
    tiles = field.reshape(shard_rows // side, side, width)
    along = jnp.einsum("ab,ibc->iac", table, tiles, precision=lax.Precision.HIGHEST)
    block = jnp.kron(jnp.eye(width // side, dtype=jnp.float32), table.T)
    return jnp.matmul(along, block, precision=lax.Precision.HIGHEST)


def inverse_tiles(spectra, table):
    side = table.shape[0]
    width = spectra.shape[2]
    along = jnp.einsum("ab,iac->ibc", table, spectra, precision=lax.Precision.HIGHEST)
    block = jnp.kron(jnp.eye(width // side, dtype=jnp.float32), table)
    result = jnp.matmul(along, block, precision=lax.Precision.HIGHEST)
    return result.reshape(spectra.shape[0] * side, width)


def one_hots(places, side, width):
    row_of = places // side
    col_of = places % side + jnp.arange(width // side, dtype=jnp.int32)[:, None] * side
    row_hot = (row_of[..., None] == jnp.arange(side, dtype=jnp.int32)).astype(jnp.float32)
    col_hot = (col_of[..., None] == jnp.arange(width, dtype=jnp.int32)).astype(jnp.float32)
    return (row_hot, col_hot)


def any_mesh(tokens, grad_out, moment, weight, next_tokens, index):
    table = cosine_table(TILE)
    width = weight.shape[1]
    partial = lax.dot_general(tokens, grad_out, (((0,), (0,)), ((), ())), preferred_element_type=jnp.float32)
    grad = lax.psum_scatter(partial.astype(jnp.bfloat16), "fsdp", scatter_dimension=0, tiled=True)
    moment_now = momentum_decay * moment[0] + grad.astype(jnp.float32)
    spectra = forward_tiles(moment_now, table)
    row_hot, col_hot = one_hots(index[0], TILE, width)
    picked = jnp.einsum("ijka,iac->ijkc", row_hot, spectra, precision=lax.Precision.HIGHEST)
    values = jnp.sum(picked * col_hot, axis=-1)
    dense = jnp.einsum("ijka,ijkc->iac", row_hot * values[..., None], col_hot, precision=lax.Precision.HIGHEST)
    new_moment = (moment_now - inverse_tiles(dense, table))[None]
    total = lax.psum(dense.astype(jnp.bfloat16), "rep").astype(jnp.float32)
    update = inverse_tiles(total, table)
    new_weight = (weight.astype(jnp.float32) - step_size * update).astype(jnp.bfloat16)
    full = lax.all_gather(new_weight, "fsdp", axis=0, tiled=True)
    next_out = jnp.dot(next_tokens, full, preferred_element_type=jnp.float32).astype(jnp.bfloat16)
    return (update, new_moment, next_out)


def solution(mesh):
    n_r, n_f = mesh.shape["rep"], mesh.shape["fsdp"]
    local = functools.partial(line_fast, n_r, n_f) if (n_r, n_f) == (8, 4) else any_mesh
    in_specs = (
        P(("rep", "fsdp"), None),
        P(("rep", "fsdp"), None),
        P("rep", "fsdp", None),
        P("fsdp", None),
        P(("rep", "fsdp"), None),
        P("rep", "fsdp", None, None),
    )
    out_specs = (P("fsdp", None), P("rep", "fsdp", None), P(("rep", "fsdp"), None))
    return jax.shard_map(local, mesh=mesh, in_specs=in_specs, out_specs=out_specs, check_vma=False)
```

```python
import functools

import jax
import jax.numpy as jnp
import numpy as np
from jax import lax
from jax.experimental import pallas as pl
from jax.experimental.pallas import tpu as pltpu
from jax.sharding import PartitionSpec as P

TILE = 64
LANES = 128

momentum_decay = 0.999
step_size = 0.005


def cosine_array(order):
    freq = np.arange(order, dtype=np.float64)[:, None]
    place = np.arange(order, dtype=np.float64)[None, :]
    table = np.sqrt(2.0 / order) * np.cos(np.pi * (2.0 * place + 1.0) * freq / (2.0 * order))
    return table * np.where(freq == 0.0, np.sqrt(0.5), 1.0)


def tables():
    block = np.kron(np.eye(2), cosine_array(TILE)).astype(np.float32)
    high = block.astype(jnp.bfloat16)
    low = (block - high.astype(np.float32)).astype(jnp.bfloat16)
    inv = np.concatenate([high.T, low.T], axis=0)
    small = [part[i : i + TILE, i : i + TILE].T for i in (0, TILE) for part in (high, low)]
    pair = np.zeros((4 * TILE, LANES), jnp.bfloat16)
    for i, part in enumerate(small):
        pair[i * TILE : (i + 1) * TILE, (i // 2) * TILE : (i // 2 + 1) * TILE] = part
    fwd = np.concatenate([high, low], axis=0)
    return jnp.asarray(inv), jnp.asarray(fwd), jnp.asarray(pair)


def split(x):
    high = x.astype(jnp.bfloat16)
    return high, (x - high.astype(jnp.float32)).astype(jnp.bfloat16)


def dot(a, b, contract=((1,), (0,))):
    return lax.dot_general(a, b, (contract, ((), ())), preferred_element_type=jnp.float32)


def hot(row, size, fill=None):
    spread = lambda x: jnp.broadcast_to(x, (16, LANES)).astype(jnp.bfloat16)
    place = spread(row)
    fill = jnp.ones((16, LANES), jnp.bfloat16) if fill is None else spread(fill)
    none = jnp.zeros((16, LANES), jnp.bfloat16)
    sub = lax.broadcasted_iota(jnp.int32, (16, LANES), 0).astype(jnp.float32)
    parts = [jnp.where((sub + 16.0 * i).astype(jnp.bfloat16) == place, fill, none) for i in range(size // 16)]
    return jnp.concatenate(parts, axis=0)


def chunk_of(slot, f):
    return jnp.where(slot < 2, jnp.where(slot == 0, 3 - 3 * (f & 1), 1 + (f & 1)), jnp.where(slot == 2, f ^ 2, f))


def partial_kernel(me, tok, grad, *outs):
    for i, out in enumerate(outs):

        @pl.when(pl.program_id(0) == i)
        def _():
            out[...] = dot(tok[...], grad[...], ((0,), (0,))).astype(out.dtype)


def partial_chunks(me, tokens, grad_out, rows):
    count = 4
    width = grad_out.shape[1]
    toks = tokens.shape[0]
    return pl.pallas_call(
        partial_kernel,
        grid_spec=pltpu.PrefetchScalarGridSpec(
            num_scalar_prefetch=1,
            grid=(count,),
            in_specs=[
                pl.BlockSpec((toks, rows), lambda s, me: (0, chunk_of(s, me[0]))),
                pl.BlockSpec((toks, width), lambda s, me: (0, 0)),
            ],
            out_specs=[pl.BlockSpec((rows, width), lambda s, me: (0, 0)) for _ in range(count)],
        ),
        out_shape=[jax.ShapeDtypeStruct((rows, width), jnp.bfloat16) for _ in range(count)],
        cost_estimate=pl.CostEstimate(
            flops=2 * count * rows * width * toks, bytes_accessed=count * rows * (width + toks) * 2, transcendentals=0
        ),
        compiler_params=pltpu.CompilerParams(vmem_limit_bytes=16 * 2**20),
    )(me, tokens, grad_out)


def idx_block(s, unit):
    return jnp.where(s == 0, 0, unit * (s - 1) + 1)


def select_kernel(groups, me, pair_ref, idx_ref, tok_ref, grad_ref, moment_ref, out_ref):
    pair = pair_ref[...]
    grad = jnp.concatenate([grad_ref[...]] * 2, axis=1)
    places = (idx_ref[...].astype(jnp.int32) & (TILE - 1)).astype(jnp.float32)
    lane = lax.broadcasted_iota(jnp.int32, (TILE, LANES), 1)
    top = lane < TILE
    even = (lane // (TILE // 2)) % 2 == 0
    none = jnp.zeros((TILE, LANES), jnp.float32)

    def spread(low_half, high, low):
        parts = [jnp.where(low_half, high, none), jnp.where(low_half, none, high)]
        parts += [jnp.where(low_half, low, none), jnp.where(low_half, none, low)]
        return jnp.concatenate(parts, axis=0)

    batch = groups

    def some_groups(g, own):
        of = range(g, g + batch)
        rows = [jnp.concatenate([hot(places[i : i + 1], TILE), hot(places[groups + i : groups + i + 1], TILE)], axis=0) for i in of]
        both = dot(pair, jnp.concatenate(rows, axis=1))
        quarters = [[both[q * TILE : (q + 1) * TILE, i * LANES : (i + 1) * LANES] for q in range(4)] for i in range(batch)]
        a2s = [spread(top, quarter[0], quarter[1]) for quarter in quarters]
        b2s = [spread(even, quarter[2], quarter[3]).astype(jnp.bfloat16) for quarter in quarters]
        gb = dot(grad, jnp.concatenate(b2s, axis=1))
        toks = [tok_ref[:, i * LANES : (i + 1) * LANES] for i in of]
        tas = [dot(jnp.concatenate([tok, tok], axis=1), a2.astype(jnp.bfloat16)) for tok, a2 in zip(toks, a2s)]
        values = [
            jnp.sum(ta * gb[:, i * LANES : (i + 1) * LANES], axis=0, keepdims=True) for i, ta in enumerate(tas)
        ]
        if own:
            parts = [split(momentum_decay * moment_ref[i * LANES : (i + 1) * LANES, :]) for i in of]
            mbs = [
                dot(jnp.concatenate([hi, hi], axis=1), b2) + dot(lo, b2[:LANES]) for (hi, lo), b2 in zip(parts, b2s)
            ]
            values = [
                value + jnp.sum(mb * (a2[:LANES] + a2[LANES:]), axis=0, keepdims=True)
                for value, mb, a2 in zip(values, mbs, a2s)
            ]
        out_ref[0, g : g + batch, :] = jnp.concatenate(values, axis=0)

    @pl.when(pl.program_id(0) == 0)
    def _():
        for g in range(0, groups, batch):
            some_groups(g, True)

    @pl.when(pl.program_id(0) != 0)
    def _():
        for g in range(0, groups, batch):
            some_groups(g, False)


def select_values(me, inv, idx, unit, tokens, grad_out, moment):
    n_f = tokens.shape[1] // moment.shape[0]
    rows = moment.shape[0]
    groups = rows // LANES
    toks = tokens.shape[0]
    width = grad_out.shape[1]
    return pl.pallas_call(
        functools.partial(select_kernel, groups),
        grid_spec=pltpu.PrefetchScalarGridSpec(
            num_scalar_prefetch=1,
            grid=(n_f,),
            in_specs=[
                pl.BlockSpec(inv.shape, lambda s, me: (0, 0)),
                pl.BlockSpec((2 * groups, LANES), lambda s, me: (idx_block(s, unit), 0)),
                pl.BlockSpec((toks, rows), lambda s, me: (0, me[0] ^ s)),
                pl.BlockSpec((toks, width), lambda s, me: (0, 0)),
                pl.BlockSpec((rows, width), lambda s, me: (0, 0)),
            ],
            out_specs=pl.BlockSpec((1, groups, LANES), lambda s, me: (me[0] ^ s, 0, 0)),
        ),
        out_shape=jax.ShapeDtypeStruct((n_f, groups, LANES), jnp.float32),
        cost_estimate=pl.CostEstimate(
            flops=2 * n_f * groups * LANES**3 * 6, bytes_accessed=4 * 2**20, transcendentals=0
        ),
        compiler_params=pltpu.CompilerParams(vmem_limit_bytes=16 * 2**20),
    )(me, inv, idx, tokens, grad_out, moment)


def moment_kernel(groups, me, inv_ref, idx_ref, val_ref, moment_ref, kept_ref, outer_ref, inner_ref, two_ref, far_ref, out_ref):
    inv = inv_ref[...]
    outer = (me[0] == 0) | (me[0] == me[1] - 1)
    step = groups // 2
    first = pl.multiple_of(pl.program_id(0) * step, step)
    row_at = idx_ref[...].astype(jnp.float32)
    upper = pl.program_id(0) > 0
    pick = lambda x: jnp.where(upper, x[step:], x[:step])
    rows, cols, worth = pick(row_at[:groups]), pick(row_at[groups:]), pick(val_ref[0])
    of = range(step)
    hots = [jnp.concatenate([hot(rows[g : g + 1], LANES), hot(cols[g : g + 1], LANES)], axis=1) for g in of]
    both = dot(inv, jnp.concatenate(hots, axis=1))
    block = lambda half, g: both[half * LANES : (half + 1) * LANES, g * LANES : (g + 1) * LANES]
    lefts = [split((block(0, 2 * g) + block(1, 2 * g)) * worth[g : g + 1, :]) for g in of]
    lefts = [jnp.concatenate([hi, hi, lo], axis=1) for hi, lo in lefts]
    rights = [jnp.concatenate([block(0, 2 * g + 1), block(1, 2 * g + 1)], axis=1).astype(jnp.bfloat16) for g in of]
    rights = [jnp.concatenate([right, right[:, :LANES]], axis=1) for right in rights]
    slabs = jnp.concatenate([dot(left, right, ((1,), (1,))) for left, right in zip(lefts, rights)], axis=0)
    wide = lambda ref: ref[...].astype(jnp.float32)
    got = wide(kept_ref) + jnp.where(outer, wide(outer_ref), wide(inner_ref)) + (wide(two_ref) + wide(far_ref))
    out_ref[...] = (momentum_decay * moment_ref[...] + got) - slabs


def new_moment_of(me, inv, idx, values, moment, *parts):
    groups = values.shape[1]
    rows, width = moment.shape
    slab = pl.BlockSpec((rows // 2, width), lambda i, me: (i, 0))
    return pl.pallas_call(
        functools.partial(moment_kernel, groups),
        grid_spec=pltpu.PrefetchScalarGridSpec(
            num_scalar_prefetch=1,
            grid=(2,),
            in_specs=[
                pl.BlockSpec(inv.shape, lambda i, me: (0, 0)),
                pl.BlockSpec((2 * groups, LANES), lambda i, me: (0, 0)),
                pl.BlockSpec((1, groups, LANES), lambda i, me: (me[0], 0, 0)),
                slab,
            ]
            + [slab for _ in parts],
            out_specs=slab,
        ),
        out_shape=jax.ShapeDtypeStruct((rows, width), jnp.float32),
        cost_estimate=pl.CostEstimate(
            flops=2 * groups * LANES**3 * 7, bytes_accessed=5 * rows * width * 4, transcendentals=0
        ),
        compiler_params=pltpu.CompilerParams(vmem_limit_bytes=16 * 2**20),
    )(me, inv, idx, values, moment, *parts)


AWAY = (0, 4, 2, 6, 1, 5, 3, 7)


def project_kernel(n_r, n_f, extra, me, inv_ref, nt_ref, weight_ref, *refs):
    pieces, (out_ref, coef_ref) = refs[:n_r], refs[n_r:]
    width = nt_ref.shape[1]
    size = width // (n_r * n_f)
    near = nt_ref[:, pl.ds(pl.multiple_of(me[0] * size * n_r, size * n_r), size * n_r)]
    total = dot(near, weight_ref[...])
    for p in range(1, n_f):
        lefts, rights = [], []
        for away, piece in zip(AWAY, pieces):
            place = (me[0] ^ p) * n_r + (me[2] ^ away)
            lefts.append(nt_ref[:, pl.ds(pl.multiple_of(place * size, size), size)])
            rights.append(piece[p * (extra + size) - size + extra : p * (extra + size) + extra, :])
        total += dot(jnp.concatenate(lefts, axis=1), jnp.concatenate(rights, axis=0))
    out_ref[...] = total
    inv = inv_ref[...]
    table = jnp.concatenate([inv[:LANES], inv[LANES:]], axis=1)
    toks = nt_ref.shape[0]
    batch = 8
    for g in range(0, width // LANES, batch):
        parts = [slice(i * LANES, (i + 1) * LANES) for i in range(g, g + batch)]
        both = dot(jnp.concatenate([nt_ref[:, part] for part in parts], axis=0), table)
        both = (both[:, :LANES] + both[:, LANES:]).astype(jnp.bfloat16)
        for i, part in enumerate(parts):
            coef_ref[:, part] = both[i * toks : (i + 1) * toks]


def project(me, inv, next_tokens, weight, pieces, extra):
    n_r = len(pieces)
    toks, width = next_tokens.shape
    n_f = width // weight.shape[0]
    out = weight.shape[1]
    full = lambda *shape: pl.BlockSpec(shape, lambda i, me: (0,) * len(shape))
    return pl.pallas_call(
        functools.partial(project_kernel, n_r, n_f, extra),
        grid_spec=pltpu.PrefetchScalarGridSpec(
            num_scalar_prefetch=1,
            grid=(1,),
            in_specs=[full(*inv.shape), full(toks, width), full(*weight.shape)] + [full(*piece.shape) for piece in pieces],
            out_specs=[full(toks, out), full(toks, width)],
        ),
        out_shape=[jax.ShapeDtypeStruct((toks, out), jnp.float32), jax.ShapeDtypeStruct((toks, width), jnp.bfloat16)],
        cost_estimate=pl.CostEstimate(
            flops=2 * toks * width * out * 3, bytes_accessed=6 * toks * width * 2, transcendentals=0
        ),
        compiler_params=pltpu.CompilerParams(vmem_limit_bytes=20 * 2**20),
    )(me, inv, next_tokens, weight, *pieces)


def merge_kernel(me, third_ref, outer_ref, out_ref):
    inner = (me[0] > 0) & (me[0] < me[1] - 1)

    @pl.when(inner)
    def _():
        out_ref[...] = (third_ref[...].astype(jnp.float32) + outer_ref[...].astype(jnp.float32)).astype(out_ref.dtype)

    @pl.when(jnp.logical_not(inner))
    def _():
        out_ref[...] = third_ref[...]


def merge(me, third, outer):
    rows, width = third.shape
    slab = pl.BlockSpec((rows // 4, width), lambda i, me: (i, 0))
    return pl.pallas_call(
        merge_kernel,
        grid_spec=pltpu.PrefetchScalarGridSpec(num_scalar_prefetch=1, grid=(4,), in_specs=[slab, slab], out_specs=slab),
        out_shape=jax.ShapeDtypeStruct((rows, width), third.dtype),
        cost_estimate=pl.CostEstimate(flops=rows * width, bytes_accessed=6 * rows * width, transcendentals=0),
    )(me, third, outer)


def total_kernel(groups, n_r, me, inv_ref, fwd_ref, coef_ref, base_ref, *refs):
    idx_refs, val_refs = refs[:n_r], refs[n_r : n_r + n_r // 2]
    up_ref, out_ref, acc_ref, sort_ref, dense_ref = refs[n_r + n_r // 2 :]
    step = pl.program_id(0)
    slot = jnp.minimum(step, 1)
    inv = inv_ref[...]
    fwd = fwd_ref[...]

    @pl.when(step == 0)
    def _():
        acc_ref[...] = jnp.zeros_like(acc_ref)

    lane = lax.broadcasted_iota(jnp.int32, (groups, LANES), 1)
    quarter = LANES // 4

    def regroup(parts):
        out = []
        for t in range(4):
            row = None
            for i, part in enumerate(parts):
                moved = part if i == t else pltpu.roll(part, (quarter * (i - t)) % LANES, 1)
                row = moved if row is None else jnp.where(lane // quarter == i, moved, row)
            out.append(row)
        return out

    for quad in range(n_r // 4):
        of = range(4 * quad, 4 * quad + 4)
        spots = [idx_refs[r][...].astype(jnp.int32) & (TILE - 1) for r in of]
        worth = [val_refs[r % (n_r // 2)][r // (n_r // 2), 0].astype(jnp.float32) for r in of]
        sets = regroup([x[:groups] for x in spots]), regroup([x[groups:] for x in spots]), regroup(worth)
        for kind, four in enumerate(sets):
            for t, rows in enumerate(four):
                sort_ref[kind, quad, t] = rows.astype(jnp.float32)

    low = lax.broadcasted_iota(jnp.int32, (TILE, LANES), 1) < TILE
    batch = 2

    def some_groups(g):
        of = range(g, g + batch)
        at = lambda kind, quad, t, i: sort_ref[kind, quad, t, i : i + 1, :]
        quads = range(n_r // 4)
        side = lambda tile: jnp.concatenate([jnp.concatenate([tile(t, q) for q in quads], axis=1) for t in range(4)], axis=0)
        lefts = [side(lambda t, q: hot(at(0, q, t, i), TILE)) for i in of]
        rights = [side(lambda t, q: hot(at(1, q, t, i), TILE, at(2, q, t, i))) for i in of]
        crosses = [dot(left, right, ((1,), (1,))) for left, right in zip(lefts, rights)]
        diagonal = lambda cross, i: jnp.where(low, cross[i : i + TILE, i : i + LANES], cross[i + TILE : i + LANES, i : i + LANES])
        denses = [jnp.concatenate([diagonal(cross, 0), diagonal(cross, LANES)], axis=0) for cross in crosses]
        for i, dense in zip(of, denses):
            dense_ref[slot, i * LANES : (i + 1) * LANES, :] = jnp.concatenate(split(dense), axis=1)

    for g in range(0, groups, batch):
        some_groups(g)

    both = dot(coef_ref[...], dense_ref[slot])
    acc_ref[...] += both[:, :LANES] + both[:, LANES:]

    c_hi, c_lo = inv[:LANES], inv[LANES:]
    f_hi, f_lo = fwd[:LANES], fwd[LANES:]
    table = jnp.concatenate([c_hi, c_lo], axis=1)
    last = jnp.concatenate([f_hi, f_lo, f_hi], axis=0)
    count = up_ref.shape[0] // LANES
    of = [pl.ds(pl.multiple_of((step * count + g) * LANES, LANES), LANES) for g in range(count)]
    parts = [dense_ref[0, part, :] for part in of]
    boths = [dot(table, jnp.concatenate([part, part], axis=0)) for part in parts]
    halves = [split(both[:, :LANES] + both[:, LANES:]) for both in boths]
    lines = jnp.concatenate([jnp.concatenate([hi, hi, lo], axis=1) for hi, lo in halves], axis=0)
    up_ref[...] = dot(lines, last)

    @pl.when(step == pl.num_programs(0) - 1)
    def _():
        s_hi, s_lo = split(acc_ref[...])
        f_hi, f_lo = fwd[:LANES], fwd[LANES:]
        moved = dot(jnp.concatenate([s_hi, s_hi, s_lo], axis=1), jnp.concatenate([f_hi, f_lo, f_hi], axis=0))
        out_ref[...] = (base_ref[...] - step_size * moved).astype(out_ref.dtype)


def totals(me, inv, fwd, coef, base, pieces, unit, sent):
    n_r, n_f = len(pieces), sent[0].shape[1]
    groups = sent[0].shape[2]
    rows = groups * LANES
    toks, width = base.shape
    return pl.pallas_call(
        functools.partial(total_kernel, groups, n_r),
        grid_spec=pltpu.PrefetchScalarGridSpec(
            num_scalar_prefetch=1,
            grid=(n_f,),
            in_specs=[
                pl.BlockSpec(inv.shape, lambda s, me: (0, 0)),
                pl.BlockSpec(fwd.shape, lambda s, me: (0, 0)),
                pl.BlockSpec((toks, rows), lambda s, me: (0, me[0] ^ s)),
                pl.BlockSpec((toks, width), lambda s, me: (0, 0)),
            ]
            + [pl.BlockSpec((2 * groups, LANES), lambda s, me: (idx_block(s, unit), 0)) for _ in pieces]
            + [pl.BlockSpec((2, 1, groups, LANES), lambda s, me: (0, me[0] ^ s, 0, 0)) for _ in sent],
            out_specs=[
                pl.BlockSpec((rows // n_f, width), lambda s, me: (s, 0)),
                pl.BlockSpec((toks, width), lambda s, me: (0, 0)),
            ],
            scratch_shapes=[
                pltpu.VMEM((toks, width), jnp.float32),
                pltpu.VMEM((3, n_r // 4, 4, groups, LANES), jnp.float32),
                pltpu.VMEM((2, rows, 2 * LANES), jnp.bfloat16),
            ],
        ),
        out_shape=[
            jax.ShapeDtypeStruct((rows, width), jnp.float32),
            jax.ShapeDtypeStruct((toks, width), jnp.bfloat16),
        ],
        cost_estimate=pl.CostEstimate(
            flops=2 * n_f * groups * LANES**3 * (n_r + 2), bytes_accessed=4 * 2**20, transcendentals=0
        ),
        compiler_params=pltpu.CompilerParams(vmem_limit_bytes=16 * 2**20),
    )(me, inv, fwd, coef, base, *pieces, *sent)


def swap(x, axis, size, mask):
    return lax.ppermute(x, axis, [(i, i ^ mask) for i in range(size)])


def fence(stage, *args):
    shapes = jax.eval_shape(stage, *args)
    other = lambda *args: jax.tree.map(lambda x: jnp.zeros(x.shape, x.dtype), shapes)
    return lax.cond(lax.axis_index("rep") < lax.axis_size("rep"), stage, other, *args)


def line_fast(n_r, n_f, tokens, grad_out, moment, weight, next_tokens, index):
    bf16 = jnp.bfloat16
    r, f = lax.axis_index("rep"), lax.axis_index("fsdp")
    me = jnp.stack([f, n_f, r]).astype(jnp.int32)
    inv, fwd, pair = tables()
    moment = moment[0]
    rows = moment.shape[0]
    groups = rows // LANES
    slice_rows = rows // n_r

    flat = index[0].reshape(groups, LANES)
    lane = jnp.arange(LANES, dtype=jnp.int32)
    row_pos = flat // TILE + (lane // TILE) * TILE
    col_pos = flat % TILE + (lane // (TILE // 2)) % 2 * TILE
    own_idx = jnp.concatenate([row_pos, col_pos], axis=0).astype(bf16)
    extra = own_idx.shape[0]
    share = lax.dynamic_slice_in_dim(weight, r * slice_rows, slice_rows, axis=0)
    held = jnp.concatenate([own_idx, share], axis=0)
    unit = held.shape[0] // extra

    held = jnp.concatenate([own_idx] + [swap(held, "fsdp", n_f, p) for p in range(1, n_f)], axis=0)
    first, second, third, kept = partial_chunks(me, tokens, grad_out, rows)
    held, first, second = lax.optimization_barrier((held, first, second))
    outer = lax.ppermute(first, "fsdp", [(0, 1), (1, 0), (2, 3), (3, 2)])
    inner = lax.ppermute(second, "fsdp", [(1, 2), (2, 1)])

    def near_stage(held):
        pieces = [swap(held, "rep", n_r, away) for away in AWAY[1 : n_r // 2]]
        return select_values(me, pair, held, unit, tokens, grad_out, moment), pieces

    values, pieces = fence(near_stage, held)
    pieces = [held] + pieces
    outer, inner = lax.optimization_barrier((outer, inner))

    def sum_stage(values, third, outer, pieces):
        parts = [swap(values, "fsdp", n_f, p) for p in range(1, n_f)]
        more = [swap(piece, "rep", n_r, 1) for piece in pieces]
        return parts, merge(me, third, outer), more

    parts, merged, more = fence(sum_stage, values, third, outer, pieces[:2])
    parts, merged, second = lax.optimization_barrier((parts, merged, second))
    two = lax.ppermute(merged, "fsdp", [(0, 2), (1, 3), (2, 0), (3, 1)])
    far = lax.ppermute(second, "fsdp", [(0, 1), (3, 2)])

    def far_stage(values, parts, pieces, more):
        summed = sum(parts, values)
        sent = summed.astype(bf16)[None]
        last = [swap(piece, "rep", n_r, 1) for piece in pieces[2:]]
        sent = jnp.concatenate([sent, swap(sent, "rep", n_r, 1)], axis=0)
        sent, last = lax.optimization_barrier((sent, last))
        sents = [sent] + [swap(sent, "rep", n_r, away) for away in AWAY[1 : n_r // 2]]
        old_out, coef = project(me, inv, next_tokens, weight, pieces + more + last, extra)
        return summed, sents, old_out, coef, last

    values, sents, old_out, coef, last = fence(far_stage, values, parts, pieces, more)
    pieces = pieces + more + last
    update, next_out = totals(me, inv, fwd, coef, old_out, pieces, unit, sents)
    update, two, far = lax.optimization_barrier((update, two, far))
    new_moment = new_moment_of(me, inv, held, values, moment, kept, outer, inner, two, far)
    return update, new_moment[None], next_out


def cosine_table(order):
    return jnp.asarray(cosine_array(order), jnp.float32)


def forward_tiles(field, table):
    side = table.shape[0]
    shard_rows, width = field.shape
    tiles = field.reshape(shard_rows // side, side, width)
    along = jnp.einsum("ab,ibc->iac", table, tiles, precision=lax.Precision.HIGHEST)
    block = jnp.kron(jnp.eye(width // side, dtype=jnp.float32), table.T)
    return jnp.matmul(along, block, precision=lax.Precision.HIGHEST)


def inverse_tiles(spectra, table):
    side = table.shape[0]
    width = spectra.shape[2]
    along = jnp.einsum("ab,iac->ibc", table, spectra, precision=lax.Precision.HIGHEST)
    block = jnp.kron(jnp.eye(width // side, dtype=jnp.float32), table)
    result = jnp.matmul(along, block, precision=lax.Precision.HIGHEST)
    return result.reshape(spectra.shape[0] * side, width)


def one_hots(places, side, width):
    row_of = places // side
    col_of = places % side + jnp.arange(width // side, dtype=jnp.int32)[:, None] * side
    row_hot = (row_of[..., None] == jnp.arange(side, dtype=jnp.int32)).astype(jnp.float32)
    col_hot = (col_of[..., None] == jnp.arange(width, dtype=jnp.int32)).astype(jnp.float32)
    return (row_hot, col_hot)


def any_mesh(tokens, grad_out, moment, weight, next_tokens, index):
    table = cosine_table(TILE)
    width = weight.shape[1]
    partial = lax.dot_general(tokens, grad_out, (((0,), (0,)), ((), ())), preferred_element_type=jnp.float32)
    grad = lax.psum_scatter(partial.astype(jnp.bfloat16), "fsdp", scatter_dimension=0, tiled=True)
    moment_now = momentum_decay * moment[0] + grad.astype(jnp.float32)
    spectra = forward_tiles(moment_now, table)
    row_hot, col_hot = one_hots(index[0], TILE, width)
    picked = jnp.einsum("ijka,iac->ijkc", row_hot, spectra, precision=lax.Precision.HIGHEST)
    values = jnp.sum(picked * col_hot, axis=-1)
    dense = jnp.einsum("ijka,ijkc->iac", row_hot * values[..., None], col_hot, precision=lax.Precision.HIGHEST)
    new_moment = (moment_now - inverse_tiles(dense, table))[None]
    total = lax.psum(dense.astype(jnp.bfloat16), "rep").astype(jnp.float32)
    update = inverse_tiles(total, table)
    new_weight = (weight.astype(jnp.float32) - step_size * update).astype(jnp.bfloat16)
    full = lax.all_gather(new_weight, "fsdp", axis=0, tiled=True)
    next_out = jnp.dot(next_tokens, full, preferred_element_type=jnp.float32).astype(jnp.bfloat16)
    return (update, new_moment, next_out)


def solution(mesh):
    n_r, n_f = mesh.shape["rep"], mesh.shape["fsdp"]
    local = functools.partial(line_fast, n_r, n_f) if (n_r, n_f) == (8, 4) else any_mesh
    in_specs = (
        P(("rep", "fsdp"), None),
        P(("rep", "fsdp"), None),
        P("rep", "fsdp", None),
        P("fsdp", None),
        P(("rep", "fsdp"), None),
        P("rep", "fsdp", None, None),
    )
    out_specs = (P("fsdp", None), P("rep", "fsdp", None), P(("rep", "fsdp"), None))
    return jax.shard_map(local, mesh=mesh, in_specs=in_specs, out_specs=out_specs, check_vma=False)
```
